32 devices in a mesh: lat: 1, lon: 32 (over z, y, x, core).
Axes of the slice: x: 2, y: 2, z: 4, core: 2. Of those that a mesh axis runs over, the one named last changes fastest.
Arguments:
- fields: bfloat16 [2, 24, 768, 256], P(None, 'lat', 'lon'), may hold values from -6 to 6
- legendre: float32 [24, 192, 8], P('lat', 'lon'), may hold values from -1.25 to 1.25
- mixing: bfloat16 [8, 256, 256], P('lat'), may hold values from -0.375 to 0.375
- cotangent: bfloat16 [8, 192, 2, 2, 256], P('lat', 'lon'), may hold values from -0.3046875 to 0.3046875
Outputs:
- mixed: bfloat16 [8, 192, 2, 2, 256], P('lat', 'lon')
- weight_grad: float32 [256, 8, 256], P('lon', 'lat')
The draws below stay inside these ranges and needn't reach their ends.
All inputs are finite; a program needn't handle non-finite values.
Results may differ from the reference program's by a relative error of at most 0.015.
Values may be sent and summed in bfloat16 or wider, within the bound.
No kernel may reach another device: no remote copies, remote signals or barrier semaphores. Data moves between devices by JAX's collectives and lax.ppermute only.
A program may use at most 64 MiB of HBM per device.

```python
import jax
import jax.numpy as jnp
from jax import lax

C = 256
B = 2
NLAT = 24
NLON = 768
M = 192
L = 8


def shard_levels(own_key, shape, shards, smallest, largest):
    factor_of = 1.0
    for axis_at, shards_of in shards:
        heights = jax.random.uniform(jax.random.fold_in(jax.random.fold_in(own_key, 6), axis_at), (shards_of,), jnp.float32, smallest / len(shards), largest / len(shards))
        factor_of = factor_of * jnp.repeat(jnp.exp(heights), shape[axis_at] // shards_of).reshape((-1,) + (1,) * (len(shape) - 1 - axis_at))
    return factor_of


def scatter_about(key, dims, deviation, reach, pieces=(), kind=jnp.bfloat16):
    values = jax.random.normal(key, dims, jnp.float32) * deviation
    if len(pieces) > 0:
        values = shard_levels(key, dims, pieces, -0.22, 0.18) * values
    return jnp.clip(values, min=-reach, max=reach).astype(kind)


def setup_inputs(seed: int = 0) -> dict:
    keys = jax.random.split(jax.random.key(seed), 5)
    return {
        "fields": scatter_about(keys[0], (B, NLAT, NLON, C), 1.0, 6.0, ((2, 32),)),
        "legendre": scatter_about(keys[1], (NLAT, M, L), NLAT ** -0.5, 1.25, ((1, 32),), jnp.float32),
        "mixing": scatter_about(keys[2], (L, C, C), C ** -0.5, 0.375),
        "cotangent": scatter_about(keys[3], (L, M, 2, B, C), ((B * M) ** -0.5), 0.3046875, ((1, 32),)),
    }


def reference(fields, legendre, mixing, cotangent):
    nlon_total = fields.shape[2]
    wave = jnp.fft.rfft(fields.astype(jnp.float32), axis=2)[:, :, :M, :]
    spectrum = jnp.stack([jnp.real(wave), jnp.imag(wave)], axis=3) * (1.0 / nlon_total ** 0.5)
    spectrum = spectrum.astype(jnp.float32)
    keep = jnp.arange(L, dtype=jnp.int32)[None, :] >= jnp.arange(M, dtype=jnp.int32)[:, None]
    basis = jnp.where(keep[None, :, :], legendre, jnp.float32(0.0))
    coef = jnp.einsum('jml,bjmpc->lmpbc', basis, spectrum, precision=lax.Precision.HIGHEST)
    coef_bf = coef.astype(jnp.bfloat16)
    mixed = jnp.einsum('lmpbc,lcd->lmpbd', coef_bf.astype(jnp.float32), mixing.astype(jnp.float32), precision=lax.Precision.HIGHEST)
    weight_grad = jnp.einsum('lmpbc,lmpbd->cld', coef_bf.astype(jnp.float32), cotangent.astype(jnp.float32), precision=lax.Precision.HIGHEST)
    return mixed.astype(jnp.bfloat16), weight_grad
```

```python
import functools
import math

import jax
import jax.numpy as jnp
from jax import lax
from jax.experimental import pallas as pl
from jax.experimental.pallas import tpu as pltpu
from jax.sharding import PartitionSpec as P

F32 = jnp.float32
BF16 = jnp.bfloat16
TILE = 8
LANES = 128
VMEM_BYTES = 32 * 1024 * 1024


def dense_shards(fields, legendre, mixing, cotangent):
    samples = fields.shape[0]
    lat_rows = fields.shape[1]
    lon_cells = fields.shape[2]
    channels = fields.shape[3]
    lon_count = lax.axis_size("lon")
    lat_count = lax.axis_size("lat")
    nlon_total = lon_cells * lon_count
    wave_dev = legendre.shape[1]
    wave_total = wave_dev * lon_count
    degrees = legendre.shape[2]
    degree_dev = degrees // lat_count
    column_rows = 2 * wave_dev * samples
    column_width = 2 * samples * channels
    positions = jnp.arange(nlon_total, dtype=jnp.int32)
    wavenums = jnp.arange(wave_total, dtype=jnp.int32)
    phase = (positions[:, None] * wavenums[None, :] % nlon_total).astype(jnp.float32) * (
        2.0 * math.pi / nlon_total
    )
    fourier = jnp.stack([jnp.cos(phase), -jnp.sin(phase)], axis=2).reshape(
        nlon_total, 2 * wave_total
    )
    fourier = fourier * (1.0 / nlon_total**0.5)
    fourier_hi = fourier.astype(jnp.bfloat16)
    fourier_lo = (fourier - fourier_hi.astype(jnp.float32)).astype(jnp.bfloat16)
    portion = lax.all_to_all(fields, "lon", split_axis=3, concat_axis=2, tiled=True)
    spectrum = jnp.einsum("bjkc,kf->jfbc", portion, fourier_hi, preferred_element_type=jnp.float32)
    spectrum = spectrum + jnp.einsum(
        "bjkc,kf->jfbc", portion, fourier_lo, preferred_element_type=jnp.float32
    )
    owned = lax.all_to_all(spectrum, "lon", split_axis=1, concat_axis=3, tiled=True)
    spectral = owned.reshape(owned.shape[0], column_rows, channels)
    wave_global = lax.axis_index("lon") * wave_dev + jnp.arange(wave_dev, dtype=jnp.int32)
    degree_ids = jnp.arange(degrees, dtype=jnp.int32)
    keep = degree_ids[None, None, :] >= wave_global[None, :, None]
    basis = jnp.where(keep, legendre, jnp.float32(0.0))
    spectral_waves = spectral.reshape(lat_rows, wave_dev, column_width)
    summed = lax.psum_scatter(
        jnp.einsum("jml,jmq->lmq", basis, spectral_waves, precision=lax.Precision.HIGHEST),
        "lat",
        scatter_dimension=0,
        tiled=True,
    )
    coef = summed.reshape(degree_dev, column_rows, channels)
    coef_bf = coef.astype(jnp.bfloat16)
    mixed = jnp.einsum("lrc,lcd->lrd", coef_bf, mixing, preferred_element_type=jnp.float32)
    mixed = mixed.astype(jnp.bfloat16).reshape(degree_dev, wave_dev, 2, samples, channels)
    cot_rows = cotangent.reshape(degree_dev, column_rows, channels)
    weight_grad = lax.psum_scatter(
        jnp.einsum("lrc,lrd->cld", coef_bf, cot_rows, preferred_element_type=jnp.float32),
        "lon",
        scatter_dimension=0,
        tiled=True,
    )
    return (mixed, weight_grad)


def put_rows(ref, first, stride, block):
    for lane in range(ref.shape[0]):
        piece = block[:, lane * LANES : (lane + 1) * LANES]
        ref[lane, pl.ds(first, block.shape[0], stride=stride), :] = piece


def take_rows(ref, first, count):
    return jnp.concatenate([ref[lane, pl.ds(first, count), :] for lane in range(ref.shape[0])], axis=1)


def fourier_kernel(nlon_total, where_ref, fields_ref, keep_ref, send_ref, total_ref):
    rows, cells, _ = fields_ref.shape[1:]
    parts = keep_ref.shape[0] // rows
    index = where_ref[0]
    width = TILE * cells
    column = lax.broadcasted_iota(jnp.int32, (parts, width), 1)
    part = lax.broadcasted_iota(jnp.int32, (parts, width), 0)
    cell = index * cells + lax.rem(column, cells)
    turn = lax.rem(cell * (part // 2) + lax.rem(part, 2) * (nlon_total // 4), nlon_total)
    wave = jnp.cos(turn.astype(F32) * (2.0 * math.pi / nlon_total)) * (1.0 / nlon_total**0.5)
    spread = (parts, TILE, width)
    own_row = (
        lax.broadcasted_iota(jnp.int32, spread, 2) // cells
        == lax.broadcasted_iota(jnp.int32, spread, 1)
    )
    wave = jnp.where(own_row, jnp.broadcast_to(wave[:, None, :], spread), 0.0)
    wave = wave.reshape(parts * TILE, width)
    wave_hi = wave.astype(BF16)
    wave_lo = (wave - wave_hi.astype(F32)).astype(BF16)
    core = lax.rem(index, 2)
    for out_ref, sample in ((send_ref, 1 - core), (keep_ref, core)):
        for first in range(0, rows, TILE):
            grid = fields_ref[sample, pl.ds(first, TILE)]
            grid = grid.astype(F32).reshape(width, grid.shape[2]).astype(BF16)
            sums = jnp.dot(wave_hi, grid, preferred_element_type=F32)
            sums = sums + jnp.dot(wave_lo, grid, preferred_element_type=F32)
            total_ref[:, pl.ds(first, TILE), :] = sums.reshape(parts, TILE, sums.shape[1])
        whole = total_ref[...].reshape(out_ref.shape)
        out_ref[...] = whole.astype(out_ref.dtype)


def legendre_kernel(rows, degrees, acc_ref, got_ref, out_ref, coef_ref):
    parts = 2 * degrees
    spec_rows = parts * rows
    cot_rows = out_ref.shape[0] - parts * degrees
    table_at = spec_rows + cot_rows
    table = acc_ref[pl.ds(table_at, acc_ref.shape[0] - table_at), :]
    table = table + got_ref[pl.ds(table_at, acc_ref.shape[0] - table_at), :].astype(F32)
    half = degrees // 2
    degree = lax.broadcasted_iota(jnp.int32, (degrees, rows), 0)
    for wave in range(degrees):
        at, lane = (wave % half) * degrees, (wave // half) * LANES
        block = table[at : at + degrees, lane : lane + LANES]
        basis = block[:, :rows] + block[:, rows : 2 * rows] + block[:, 2 * rows : 3 * rows]
        basis = jnp.where(degree >= wave, basis, 0.0)
        for part in (2 * wave, 2 * wave + 1):
            here = pl.ds(part * rows, rows)
            spec = acc_ref[here, :] + got_ref[here, :].astype(F32)
            sums = jnp.dot(
                basis, spec, preferred_element_type=F32, precision=lax.Precision.HIGHEST
            )
            put_rows(coef_ref, part, parts, sums)
    out_ref[pl.ds(0, parts * degrees), :] = take_rows(coef_ref, 0, parts * degrees).astype(BF16)
    here = pl.ds(spec_rows, cot_rows)
    there = pl.ds(parts * degrees, cot_rows)
    out_ref[there, :] = (acc_ref[here, :] + got_ref[here, :].astype(F32)).astype(BF16)


def mixing_kernel(
    wave_dev, samples, where_ref, mine_ref, other_ref, mixing_ref, mixed_ref, grad_ref, coef_ref, cot_ref
):
    degrees, channels = mixing_ref.shape[:2]
    parts = 2 * degrees
    coef_rows = parts * degrees
    per_degree = parts * samples
    index = where_ref[0]
    core = lax.rem(index, 2)
    terms = coef_rows * samples
    spare = coef_ref.shape[1] - terms
    put_rows(coef_ref, terms, 1, jnp.zeros((spare, channels), F32))
    mine, other = mine_ref[...].astype(F32), other_ref[...].astype(F32)
    for sample in range(samples):
        held = jnp.where(core == sample, mine, other)
        put_rows(coef_ref, sample, samples, held[:coef_rows])
        for group in range(degrees // 2 + 1):
            for part in range(2):
                at = coef_rows + (2 * group + part) * degrees
                block = held[at : at + degrees]
                row = (2 * group + part) * samples + sample
                put_rows(cot_ref, row, per_degree, block)
                if 0 < group < degrees - group:
                    row = (2 * (degrees - group) + part) * samples + sample
                    turned = pltpu.roll(block, degrees - group, 0)
                    put_rows(cot_ref, row, per_degree, turned)

    block_rows = 2 * wave_dev * samples
    offset = index * block_rows
    last = (per_degree - 1) // block_rows * block_rows
    start = jnp.minimum(offset, last)
    inside = lax.broadcasted_iota(jnp.int32, (block_rows, channels), 0) + offset < per_degree
    for degree in range(degrees):
        first = pl.multiple_of(degree * per_degree + start, TILE)
        block = jnp.where(inside, take_rows(coef_ref, first, block_rows), 0.0).astype(BF16)
        mixed = jnp.dot(block, mixing_ref[degree], preferred_element_type=F32)
        mixed_ref[degree] = mixed.astype(BF16)

    own = grad_ref.shape[0]
    channel = lax.broadcasted_iota(jnp.int32, (own, channels), 1)
    row = lax.broadcasted_iota(jnp.int32, (own, channels), 0)
    pick = jnp.where(channel == index * own + row, 1.0, 0.0).astype(BF16)
    coef = take_rows(coef_ref, 0, terms).astype(BF16)
    turned = lax.dot_general(
        pick, coef, (((1,), (1,)), ((), ())), preferred_element_type=F32
    )
    spread = (own, degrees, terms)
    of_degree = (
        lax.broadcasted_iota(jnp.int32, spread, 2) // per_degree
        == lax.broadcasted_iota(jnp.int32, spread, 1)
    )
    turned = jnp.where(of_degree, jnp.broadcast_to(turned[:, None, :], spread), 0.0)
    turned = turned.reshape(own * degrees, terms).astype(BF16)
    grad = jnp.dot(turned, take_rows(cot_ref, 0, terms).astype(BF16), preferred_element_type=F32)
    grad_ref[...] = grad.reshape(own, degrees, channels)


def pack_rows(legendre, cotangent, index, core):
    wave_dev, degrees = legendre.shape[1:]
    rows = legendre.shape[0]
    channels = cotangent.shape[4]

    def of_wave(array, wave):
        return jnp.where(index == wave // wave_dev, array[:, wave % wave_dev], 0)

    half = degrees // 2
    table = jnp.stack([of_wave(legendre, wave) for wave in range(degrees)], axis=0)
    table = table.transpose(0, 2, 1).reshape(2, half * degrees, rows)
    high = lax.reduce_precision(table, 8, 7)
    middle = lax.reduce_precision(table - high, 8, 7)
    low = table - high - middle
    pieces = jnp.concatenate([high, middle, low], axis=2)
    pieces = jnp.pad(pieces, ((0, 0), (0, 0), (0, channels // 2 - 3 * rows)))
    pieces = jnp.concatenate([pieces[0], pieces[1]], axis=1).astype(BF16)

    groups = []
    for group in range(half + 1):
        block = of_wave(cotangent, group)
        if 0 < group < degrees - group:
            rest = of_wave(cotangent, degrees - group)
            block = jnp.concatenate([rest[degrees - group :], block[group:]], axis=0)
        groups.append(block)
    packed = jnp.stack(groups, axis=0).transpose(3, 0, 2, 1, 4)
    packed = packed.reshape(packed.shape[0], (half + 1) * 2 * degrees, channels)
    mine = jnp.where(core == 0, packed[0], packed[1])
    other = jnp.where(core == 0, packed[1], packed[0])
    return jnp.concatenate([mine, pieces], axis=0), jnp.concatenate([other, pieces], axis=0)


def sparse_shards(fields, legendre, mixing, cotangent):
    samples, rows, cells, channels = fields.shape
    lon_count = lax.axis_size("lon")
    wave_dev, degrees = legendre.shape[1:]
    parts = 2 * degrees
    spec_rows = parts * rows
    index = lax.axis_index("lon")
    core = lax.rem(index, 2)
    where = index.reshape(1).astype(jnp.int32)
    whole = pl.BlockSpec(memory_space=pltpu.VMEM)
    scalar = pl.BlockSpec(memory_space=pltpu.SMEM)
    params = pltpu.CompilerParams(vmem_limit_bytes=VMEM_BYTES)

    keep, send = pl.pallas_call(
        functools.partial(fourier_kernel, cells * lon_count),
        out_shape=(
            jax.ShapeDtypeStruct((spec_rows, channels), F32),
            jax.ShapeDtypeStruct((spec_rows, channels), BF16),
        ),
        in_specs=[scalar, whole],
        out_specs=(whole, whole),
        scratch_shapes=[pltpu.VMEM((parts, rows, channels), F32)],
        compiler_params=params,
    )(where, fields)

    def exchange(array, bits):
        pairs = [(i, i ^ bits[i % 2]) for i in range(lon_count)]
        return lax.ppermute(array, "lon", pairs)

    mine, other = pack_rows(legendre, cotangent, index, core)
    got = exchange(send, (1, 1))
    extra = exchange(other, (1, 1))
    acc = jnp.concatenate(
        [keep + got.astype(F32), mine.astype(F32) + extra.astype(F32)], axis=0
    )
    bits = [1 << k for k in range(1, lon_count.bit_length() - 1)]
    shift = len(bits) // 2
    orders = list(zip(bits, bits[shift:] + bits[:shift]))
    for step, order in enumerate(orders):
        got = exchange(acc.astype(BF16), order)
        if step < len(orders) - 1:
            acc = acc + got.astype(F32)

    cot_rows = (degrees // 2 + 1) * parts
    pay_rows = parts * degrees + cot_rows
    pay = pl.pallas_call(
        functools.partial(legendre_kernel, rows, degrees),
        out_shape=jax.ShapeDtypeStruct((pay_rows, channels), BF16),
        in_specs=[whole, whole],
        out_specs=whole,
        scratch_shapes=[pltpu.VMEM((channels // LANES, parts * degrees, LANES), F32)],
        compiler_params=params,
    )(acc, got)
    paid = exchange(pay, (1, 1))

    block_rows = 2 * wave_dev * samples
    terms = parts * degrees * samples
    mixed, grad = pl.pallas_call(
        functools.partial(mixing_kernel, wave_dev, samples),
        out_shape=(
            jax.ShapeDtypeStruct((degrees, block_rows, channels), BF16),
            jax.ShapeDtypeStruct((channels // lon_count, degrees, channels), F32),
        ),
        in_specs=[scalar, whole, whole, whole],
        out_specs=(whole, whole),
        scratch_shapes=[
            pltpu.VMEM((channels // LANES, terms + block_rows, LANES), F32),
            pltpu.VMEM((channels // LANES, terms, LANES), F32),
        ],
        compiler_params=params,
    )(where, pay, paid, mixing)
    return mixed.reshape(degrees, wave_dev, 2, samples, channels), grad


def few_waves(mesh, fields, legendre):
    samples, rows, longitudes, channels = fields.shape
    waves, degrees = legendre.shape[1:]
    count = mesh.shape["lon"]
    return (
        mesh.shape["lat"] == 1
        and samples == 2
        and count >= 4
        and count & (count - 1) == 0
        and degrees == TILE
        and degrees <= waves
        and rows % TILE == 0
        and 3 * rows <= LANES
        and channels == 2 * LANES
        and channels // count == TILE
        and longitudes % 4 == 0
        and (4 * waves // count) % TILE == 0
    )


def solution(mesh):
    placed = (
        P(None, "lat", "lon", None),
        P("lat", "lon", None),
        P("lat", None, None),
        P("lat", "lon", None, None, None),
    )

    def program(fields, legendre, mixing, cotangent):
        body = sparse_shards if few_waves(mesh, fields, legendre) else dense_shards
        return jax.shard_map(
            body,
            mesh=mesh,
            in_specs=placed,
            out_specs=(P("lat", "lon", None, None, None), P("lon", "lat", None)),
            check_vma=False,
        )(fields, legendre, mixing, cotangent)

    return program
```

```python
import functools
import math

import jax
import jax.numpy as jnp
from jax import lax
from jax.experimental import pallas as pl
from jax.experimental.pallas import tpu as pltpu
from jax.sharding import PartitionSpec as P

F32 = jnp.float32
BF16 = jnp.bfloat16
TILE = 8
LANES = 128
VMEM_BYTES = 32 * 1024 * 1024


def dense_shards(fields, legendre, mixing, cotangent):
    samples = fields.shape[0]
    lat_rows = fields.shape[1]
    lon_cells = fields.shape[2]
    channels = fields.shape[3]
    lon_count = lax.axis_size("lon")
    lat_count = lax.axis_size("lat")
    nlon_total = lon_cells * lon_count
    wave_dev = legendre.shape[1]
    wave_total = wave_dev * lon_count
    degrees = legendre.shape[2]
    degree_dev = degrees // lat_count
    column_rows = 2 * wave_dev * samples
    column_width = 2 * samples * channels
    positions = jnp.arange(nlon_total, dtype=jnp.int32)
    wavenums = jnp.arange(wave_total, dtype=jnp.int32)
    phase = (positions[:, None] * wavenums[None, :] % nlon_total).astype(jnp.float32) * (
        2.0 * math.pi / nlon_total
    )
    fourier = jnp.stack([jnp.cos(phase), -jnp.sin(phase)], axis=2).reshape(
        nlon_total, 2 * wave_total
    )
    fourier = fourier * (1.0 / nlon_total**0.5)
    fourier_hi = fourier.astype(jnp.bfloat16)
    fourier_lo = (fourier - fourier_hi.astype(jnp.float32)).astype(jnp.bfloat16)
    portion = lax.all_to_all(fields, "lon", split_axis=3, concat_axis=2, tiled=True)
    spectrum = jnp.einsum("bjkc,kf->jfbc", portion, fourier_hi, preferred_element_type=jnp.float32)
    spectrum = spectrum + jnp.einsum(
        "bjkc,kf->jfbc", portion, fourier_lo, preferred_element_type=jnp.float32
    )
    owned = lax.all_to_all(spectrum, "lon", split_axis=1, concat_axis=3, tiled=True)
    spectral = owned.reshape(owned.shape[0], column_rows, channels)
    wave_global = lax.axis_index("lon") * wave_dev + jnp.arange(wave_dev, dtype=jnp.int32)
    degree_ids = jnp.arange(degrees, dtype=jnp.int32)
    keep = degree_ids[None, None, :] >= wave_global[None, :, None]
    basis = jnp.where(keep, legendre, jnp.float32(0.0))
    spectral_waves = spectral.reshape(lat_rows, wave_dev, column_width)
    summed = lax.psum_scatter(
        jnp.einsum("jml,jmq->lmq", basis, spectral_waves, precision=lax.Precision.HIGHEST),
        "lat",
        scatter_dimension=0,
        tiled=True,
    )
    coef = summed.reshape(degree_dev, column_rows, channels)
    coef_bf = coef.astype(jnp.bfloat16)
    mixed = jnp.einsum("lrc,lcd->lrd", coef_bf, mixing, preferred_element_type=jnp.float32)
    mixed = mixed.astype(jnp.bfloat16).reshape(degree_dev, wave_dev, 2, samples, channels)
    cot_rows = cotangent.reshape(degree_dev, column_rows, channels)
    weight_grad = lax.psum_scatter(
        jnp.einsum("lrc,lrd->cld", coef_bf, cot_rows, preferred_element_type=jnp.float32),
        "lon",
        scatter_dimension=0,
        tiled=True,
    )
    return (mixed, weight_grad)


def put_rows(ref, first, stride, block):
    for lane in range(ref.shape[0]):
        piece = block[:, lane * LANES : (lane + 1) * LANES]
        ref[lane, pl.ds(first, block.shape[0], stride=stride), :] = piece


def take_rows(ref, first, count):
    return jnp.concatenate([ref[lane, pl.ds(first, count), :] for lane in range(ref.shape[0])], axis=1)


def fourier_kernel(nlon_total, where_ref, fields_ref, first_ref, second_ref, send_ref, total_ref):
    rows, cells, _ = fields_ref.shape[1:]
    parts = send_ref.shape[0] // rows
    index = where_ref[0]
    width = TILE * cells
    column = lax.broadcasted_iota(jnp.int32, (parts, width), 1)
    part = lax.broadcasted_iota(jnp.int32, (parts, width), 0)
    cell = index * cells + lax.rem(column, cells)
    turn = lax.rem(cell * (part // 2) + lax.rem(part, 2) * (nlon_total // 4), nlon_total)
    wave = jnp.cos(turn.astype(F32) * (2.0 * math.pi / nlon_total)) * (1.0 / nlon_total**0.5)
    spread = (parts, TILE, width)
    own_row = (
        lax.broadcasted_iota(jnp.int32, spread, 2) // cells
        == lax.broadcasted_iota(jnp.int32, spread, 1)
    )
    wave = jnp.where(own_row, jnp.broadcast_to(wave[:, None, :], spread), 0.0)
    wave = wave.reshape(parts * TILE, width)
    wave_hi = wave.astype(BF16)
    wave_lo = (wave - wave_hi.astype(F32)).astype(BF16)
    core = lax.rem(index, 2)
    for sample in (1 - core, core):
        for first in range(0, rows, TILE):
            grid = fields_ref[sample, pl.ds(first, TILE)]
            grid = grid.astype(F32).reshape(width, grid.shape[2]).astype(BF16)
            sums = jnp.dot(wave_hi, grid, preferred_element_type=F32)
            sums = sums + jnp.dot(wave_lo, grid, preferred_element_type=F32)
            total_ref[:, pl.ds(first, TILE), :] = sums.reshape(parts, TILE, sums.shape[1])
        if sample is not core:
            send_ref[...] = total_ref[...].reshape(send_ref.shape).astype(BF16)
    cut = first_ref.shape[0] // rows
    first_ref[...] = total_ref[pl.ds(0, cut)].reshape(first_ref.shape)
    second_ref[...] = total_ref[pl.ds(cut, parts - cut)].reshape(second_ref.shape)


def legendre_kernel(
    rows, first_ref, first_got_ref, second_ref, second_got_ref, out_ref
):
    degrees = TILE
    groups = degrees // 2 + 1
    first = first_ref[...] + first_got_ref[...].astype(F32)
    second = second_ref[...] + second_got_ref[...].astype(F32)
    spec_rows = 2 * degrees * rows
    spec = jnp.concatenate([first, second], axis=0)
    packed = groups * 2 * degrees
    table = spec[spec_rows + packed :]
    coefs = []
    for part in range(2):
        for group in range(groups):
            at, lane = group // 2 * degrees, group % 2 * LANES
            basis = table[at : at + degrees, lane : lane + LANES]
            basis = basis[:, : 2 * rows] + basis[:, 2 * rows : 4 * rows]
            partner = degrees - group if 0 < group < degrees - group else group
            low = (2 * group + part) * rows
            high = (2 * partner + part) * rows
            block = jnp.concatenate([spec[low : low + rows], spec[high : high + rows]], axis=0)
            coefs.append(
                jnp.dot(basis, block, preferred_element_type=F32, precision=lax.Precision.HIGHEST)
            )
    coefs.append(spec[spec_rows : spec_rows + packed])
    out_ref[...] = jnp.concatenate(coefs, axis=0).astype(BF16)


def mixing_kernel(
    wave_dev, samples, where_ref, mine_ref, other_ref, mixing_ref, mixed_ref, grad_ref, coef_ref
):
    degrees, channels = mixing_ref.shape[:2]
    groups = degrees // 2 + 1
    slots = 2 * groups * degrees
    terms = slots * samples
    index = where_ref[0]
    core = lax.rem(index, 2)
    mine, other = mine_ref[...].astype(F32), other_ref[...].astype(F32)
    held = [jnp.where(core == k, mine, other) for k in range(2)]
    for sample in range(samples):
        put_rows(coef_ref, sample, samples, held[sample][:slots])
    coef = take_rows(coef_ref, 0, terms).astype(BF16)
    cot = jnp.concatenate([held[0][slots:], held[1][slots:]], axis=0).astype(BF16)

    block_rows = 2 * wave_dev * samples
    shape = (degrees * block_rows, terms)
    row = lax.broadcasted_iota(jnp.int32, shape, 0)
    degree = row // block_rows
    wave = index * wave_dev + row % block_rows // (2 * samples)
    group = jnp.where(wave < groups, wave, degrees - wave)
    place = jnp.where(wave < groups, degree, degree - wave)
    term = ((row // samples % 2 * groups + group) * degrees + place) * samples + row % samples
    term = jnp.where(degree >= wave, term, -1)
    chosen = jnp.where(lax.broadcasted_iota(jnp.int32, shape, 1) == term, 1.0, 0.0).astype(BF16)
    lhs = jnp.dot(chosen, coef, preferred_element_type=F32)
    for degree in range(degrees):
        block = lhs[degree * block_rows : (degree + 1) * block_rows].astype(BF16)
        mixed = jnp.dot(block, mixing_ref[degree], preferred_element_type=F32)
        mixed_ref[degree] = mixed.astype(BF16)

    own = grad_ref.shape[0]
    channel = lax.broadcasted_iota(jnp.int32, (own, channels), 1)
    row = lax.broadcasted_iota(jnp.int32, (own, channels), 0)
    pick = jnp.where(channel == index * own + row, 1.0, 0.0).astype(BF16)
    turned = lax.dot_general(
        pick, coef, (((1,), (1,)), ((), ())), preferred_element_type=F32
    )
    spread = (own, degrees, terms)
    slot = lax.broadcasted_iota(jnp.int32, spread, 2) // samples
    place, group = slot % degrees, slot // degrees % groups
    degree = jnp.where(place >= group, place, place + degrees - group)
    of_degree = degree == lax.broadcasted_iota(jnp.int32, spread, 1)
    turned = jnp.where(of_degree, jnp.broadcast_to(turned[:, None, :], spread), 0.0)
    turned = turned.reshape(own * degrees, terms).astype(BF16)
    grad = jnp.dot(turned, cot, preferred_element_type=F32)
    grad_ref[...] = grad.reshape(own, degrees, channels)


def pack_rows(legendre, cotangent, index, core):
    wave_dev, degrees = legendre.shape[1:]
    rows = legendre.shape[0]
    channels = cotangent.shape[4]
    half = degrees // 2

    def of_wave(array, wave):
        return jnp.where(index == wave // wave_dev, array[:, wave % wave_dev], 0)

    tables = []
    degree = jnp.arange(degrees, dtype=jnp.int32)[:, None]
    for group in range(half + 1):
        block = jnp.where(degree >= group, of_wave(legendre, group).T, 0)
        rest = jnp.zeros_like(block)
        if 0 < group < degrees - group:
            rest = jnp.roll(of_wave(legendre, degrees - group).T, group, axis=0)
            rest = jnp.where(degree < group, rest, 0)
        tables.append(jnp.concatenate([block, rest], axis=1))
    if len(tables) % 2:
        tables.append(jnp.zeros_like(tables[0]))
    table = jnp.stack(tables, axis=0).reshape(len(tables) // 2, 2, degrees, 2 * rows)
    table = table.transpose(0, 2, 1, 3)
    high = lax.reduce_precision(table, 8, 7)
    table = jnp.concatenate([high, table - high], axis=3)
    table = jnp.pad(table, ((0, 0), (0, 0), (0, 0), (0, LANES - 4 * rows)))
    table = table.reshape(-1, channels).astype(BF16)

    groups = []
    for group in range(half + 1):
        block = of_wave(cotangent, group)
        if 0 < group < degrees - group:
            rest = of_wave(cotangent, degrees - group)
            block = jnp.concatenate([rest[degrees - group :], block[group:]], axis=0)
        groups.append(block)
    packed = jnp.stack(groups, axis=0)
    mine = jnp.where(core == 0, packed[:, :, 0], packed[:, :, 1]).reshape(-1, channels)
    other = jnp.where(core == 0, packed[:, :, 1], packed[:, :, 0]).reshape(-1, channels)
    return jnp.concatenate([mine, table], axis=0), jnp.concatenate([other, table], axis=0)


def sparse_shards(fields, legendre, mixing, cotangent):
    samples, rows, cells, channels = fields.shape
    lon_count = lax.axis_size("lon")
    wave_dev, degrees = legendre.shape[1:]
    parts = 2 * degrees
    spec_rows = parts * rows
    packed_rows = (degrees // 2 + 1) * parts
    index = lax.axis_index("lon")
    core = lax.rem(index, 2)
    where = index.reshape(1).astype(jnp.int32)
    whole = pl.BlockSpec(memory_space=pltpu.VMEM)
    scalar = pl.BlockSpec(memory_space=pltpu.SMEM)
    params = pltpu.CompilerParams(vmem_limit_bytes=VMEM_BYTES)

    def exchange(array, even, odd):
        pairs = [(i, i ^ (odd if i % 2 else even)) for i in range(lon_count)]
        return lax.ppermute(array, "lon", pairs)

    cut = (parts // 2 + 2) * rows
    keep_a, keep_b, send = pl.pallas_call(
        functools.partial(fourier_kernel, cells * lon_count),
        out_shape=(
            jax.ShapeDtypeStruct((cut, channels), F32),
            jax.ShapeDtypeStruct((spec_rows - cut, channels), F32),
            jax.ShapeDtypeStruct((spec_rows, channels), BF16),
        ),
        in_specs=[scalar, whole],
        out_specs=(whole, whole, whole),
        scratch_shapes=[pltpu.VMEM((parts, rows, channels), F32)],
        compiler_params=params,
    )(where, fields)

    got = exchange(send, 1, 1)
    extra, other = pack_rows(legendre, cotangent, index, core)
    extra = extra + exchange(other, 1, 1)
    acc_a = keep_a + got[:cut].astype(F32)
    acc_b = jnp.concatenate([keep_b + got[cut:].astype(F32), extra.astype(F32)], axis=0)
    orders_a, orders_b = hop_orders(lon_count)
    for step, (hops_a, hops_b) in enumerate(zip(orders_a, orders_b)):
        got_a = exchange(acc_a.astype(BF16), *hops_a)
        got_b = exchange(acc_b.astype(BF16), *hops_b)
        if step < len(orders_a) - 1:
            acc_a = acc_a + got_a.astype(F32)
            acc_b = acc_b + got_b.astype(F32)

    mine = pl.pallas_call(
        functools.partial(legendre_kernel, rows),
        out_shape=jax.ShapeDtypeStruct((2 * packed_rows, channels), BF16),
        in_specs=[whole] * 4,
        out_specs=whole,
        compiler_params=params,
    )(acc_a, got_a, acc_b, got_b)
    other = exchange(mine, 1, 1)

    block_rows = 2 * wave_dev * samples
    mixed, grad = pl.pallas_call(
        functools.partial(mixing_kernel, wave_dev, samples),
        out_shape=(
            jax.ShapeDtypeStruct((degrees, block_rows, channels), BF16),
            jax.ShapeDtypeStruct((channels // lon_count, degrees, channels), F32),
        ),
        in_specs=[scalar] + [whole] * 3,
        out_specs=(whole, whole),
        scratch_shapes=[pltpu.VMEM((channels // LANES, packed_rows * samples, LANES), F32)],
        compiler_params=params,
    )(where, mine, other, mixing)
    return mixed.reshape(degrees, wave_dev, 2, samples, channels), grad


def hop_orders(lon_count):
    bits = [1 << k for k in range(1, lon_count.bit_length() - 1)]
    bits[-1] += bits[-2]
    half = len(bits) // 2
    near, far = bits[:half], bits[half:]
    chain_a = list(zip(near + far, far + near))
    chain_b = list(zip(near[::-1] + far[::-1], far[::-1] + near[::-1]))
    return chain_a, chain_b


def few_waves(mesh, fields, legendre):
    samples, rows, longitudes, channels = fields.shape
    waves, degrees = legendre.shape[1:]
    count = mesh.shape["lon"]
    return (
        mesh.shape["lat"] == 1
        and samples == 2
        and count >= 8
        and count & (count - 1) == 0
        and degrees == TILE
        and degrees <= waves
        and rows % TILE == 0
        and 4 * rows <= LANES
        and channels == 2 * LANES
        and channels // count == TILE
        and longitudes % 4 == 0
        and (4 * waves // count) % TILE == 0
    )


def solution(mesh):
    placed = (
        P(None, "lat", "lon", None),
        P("lat", "lon", None),
        P("lat", None, None),
        P("lat", "lon", None, None, None),
    )

    def program(fields, legendre, mixing, cotangent):
        body = sparse_shards if few_waves(mesh, fields, legendre) else dense_shards
        return jax.shard_map(
            body,
            mesh=mesh,
            in_specs=placed,
            out_specs=(P("lat", "lon", None, None, None), P("lon", "lat", None)),
            check_vma=False,
        )(fields, legendre, mixing, cotangent)

    return program
```

```python
import functools
import math

import jax
import jax.numpy as jnp
from jax import lax
from jax.experimental import pallas as pl
from jax.experimental.pallas import tpu as pltpu
from jax.sharding import PartitionSpec as P

F32 = jnp.float32
BF16 = jnp.bfloat16
TILE = 8
LANES = 128
VMEM_BYTES = 32 * 1024 * 1024


def dense_shards(fields, legendre, mixing, cotangent):
    samples = fields.shape[0]
    lat_rows = fields.shape[1]
    lon_cells = fields.shape[2]
    channels = fields.shape[3]
    lon_count = lax.axis_size("lon")
    lat_count = lax.axis_size("lat")
    nlon_total = lon_cells * lon_count
    wave_dev = legendre.shape[1]
    wave_total = wave_dev * lon_count
    degrees = legendre.shape[2]
    degree_dev = degrees // lat_count
    column_rows = 2 * wave_dev * samples
    column_width = 2 * samples * channels
    positions = jnp.arange(nlon_total, dtype=jnp.int32)
    wavenums = jnp.arange(wave_total, dtype=jnp.int32)
    phase = (positions[:, None] * wavenums[None, :] % nlon_total).astype(jnp.float32) * (
        2.0 * math.pi / nlon_total
    )
    fourier = jnp.stack([jnp.cos(phase), -jnp.sin(phase)], axis=2).reshape(
        nlon_total, 2 * wave_total
    )
    fourier = fourier * (1.0 / nlon_total**0.5)
    fourier_hi = fourier.astype(jnp.bfloat16)
    fourier_lo = (fourier - fourier_hi.astype(jnp.float32)).astype(jnp.bfloat16)
    portion = lax.all_to_all(fields, "lon", split_axis=3, concat_axis=2, tiled=True)
    spectrum = jnp.einsum("bjkc,kf->jfbc", portion, fourier_hi, preferred_element_type=jnp.float32)
    spectrum = spectrum + jnp.einsum(
        "bjkc,kf->jfbc", portion, fourier_lo, preferred_element_type=jnp.float32
    )
    owned = lax.all_to_all(spectrum, "lon", split_axis=1, concat_axis=3, tiled=True)
    spectral = owned.reshape(owned.shape[0], column_rows, channels)
    wave_global = lax.axis_index("lon") * wave_dev + jnp.arange(wave_dev, dtype=jnp.int32)
    degree_ids = jnp.arange(degrees, dtype=jnp.int32)
    keep = degree_ids[None, None, :] >= wave_global[None, :, None]
    basis = jnp.where(keep, legendre, jnp.float32(0.0))
    spectral_waves = spectral.reshape(lat_rows, wave_dev, column_width)
    summed = lax.psum_scatter(
        jnp.einsum("jml,jmq->lmq", basis, spectral_waves, precision=lax.Precision.HIGHEST),
        "lat",
        scatter_dimension=0,
        tiled=True,
    )
    coef = summed.reshape(degree_dev, column_rows, channels)
    coef_bf = coef.astype(jnp.bfloat16)
    mixed = jnp.einsum("lrc,lcd->lrd", coef_bf, mixing, preferred_element_type=jnp.float32)
    mixed = mixed.astype(jnp.bfloat16).reshape(degree_dev, wave_dev, 2, samples, channels)
    cot_rows = cotangent.reshape(degree_dev, column_rows, channels)
    weight_grad = lax.psum_scatter(
        jnp.einsum("lrc,lrd->cld", coef_bf, cot_rows, preferred_element_type=jnp.float32),
        "lon",
        scatter_dimension=0,
        tiled=True,
    )
    return (mixed, weight_grad)


def tile_slots(degrees):
    slots = []
    for group in range(degrees // 2 + 1):
        for place in range(degrees):
            if place >= group:
                slots.append((group, place))
            elif group < degrees - group:
                slots.append((degrees - group, place + degrees - group))
            else:
                slots.append(None)
    return slots


def packed_tiles(wave_dev, index, cots, legendre_ref, table_ref):
    degrees, rows = legendre_ref.shape[1:]
    slots = tile_slots(degrees)
    row = lax.broadcasted_iota(jnp.int32, (TILE, LANES), 0)
    zeros = jnp.zeros((TILE, LANES), F32)
    owned = [index == owner for owner in range((degrees - 1) // wave_dev + 1)]

    def cotangent(slot):
        if slot is None:
            return zeros
        wave, degree = slot
        at = (degree * wave_dev + wave % wave_dev) * TILE
        return jnp.where(owned[wave // wave_dev], cots[at : at + TILE], 0.0)

    upper = row < TILE // 2
    parts = ([], [])
    for pair in range(len(slots) // 2):
        one, two = cotangent(slots[2 * pair]), cotangent(slots[2 * pair + 1])
        parts[0].append(jnp.where(upper, one, pltpu.roll(two, TILE // 2, 0)))
        parts[1].append(jnp.where(upper, pltpu.roll(one, TILE // 2, 0), two))

    table_ref[...] = jnp.zeros(table_ref.shape, F32)
    table_ref[:, :, pl.ds(0, rows)] = legendre_ref[...]

    def basis(wave):
        block = jnp.where(owned[wave // wave_dev], table_ref[wave % wave_dev], 0.0)
        return jnp.where(row >= wave, block, 0.0)

    groups = degrees // 2 + 1
    tables = []
    for group in range(groups):
        block = basis(group)
        if 0 < group < degrees - group:
            rest = pltpu.roll(basis(degrees - group), group, 0)
            block = block + pltpu.roll(rest, rows, 1)
        high = block.astype(BF16).astype(F32)
        tables.append(high + pltpu.roll(block - high, 2 * rows, 1))
    tables += [zeros] * (groups % 2)

    half = len(slots) // 4
    whole = []
    for tiles in parts:
        lanes = [tiles[lane * half : (lane + 1) * half] + tables[lane::2] for lane in range(2)]
        whole.append(jnp.concatenate([jnp.concatenate(lane, axis=0) for lane in lanes], axis=1))
    return whole


def fourier_kernel(
    nlon_total,
    where_ref,
    fields_ref,
    legendre_ref,
    cot_ref,
    first_ref,
    second_ref,
    send_ref,
    grid_ref,
    values_ref,
    cots_ref,
    total_ref,
    table_ref,
    sems,
):
    rows, cells, channels = fields_ref.shape[1:]
    wave_dev, degrees = legendre_ref.shape[:2]
    parts = 2 * degrees
    spec_rows = parts * rows
    index = where_ref[0]
    core = lax.rem(index, 2)
    chunks = [(k, first) for k in range(2) for first in range(0, rows, TILE)]
    copies = []
    for slot, (k, first) in enumerate(chunks):
        sample = 1 - core if k == 0 else core
        copies.append(
            pltpu.make_async_copy(
                fields_ref.at[sample, pl.ds(first, TILE)], grid_ref.at[slot], sems.at[slot]
            )
        )
    copies.append(pltpu.make_async_copy(legendre_ref, values_ref, sems.at[len(chunks)]))
    copies.append(pltpu.make_async_copy(cot_ref, cots_ref, sems.at[len(chunks) + 1]))
    for copy in copies:
        copy.start()
    width = TILE * cells
    column = lax.broadcasted_iota(jnp.int32, (parts, width), 1)
    part = lax.broadcasted_iota(jnp.int32, (parts, width), 0)
    cell = index * cells + lax.rem(column, cells)
    turn = lax.rem(cell * (part // 2) + lax.rem(part, 2) * (nlon_total // 4), nlon_total)
    wave = jnp.cos(turn.astype(F32) * (2.0 * math.pi / nlon_total)) * (1.0 / nlon_total**0.5)
    spread = (parts, TILE, width)
    own_row = (
        lax.broadcasted_iota(jnp.int32, spread, 2) // cells
        == lax.broadcasted_iota(jnp.int32, spread, 1)
    )
    wave = jnp.where(own_row, jnp.broadcast_to(wave[:, None, :], spread), 0.0)
    wave = wave.reshape(parts * TILE, width)
    wave_hi = wave.astype(BF16)
    wave_lo = (wave - wave_hi.astype(F32)).astype(BF16)
    cut = first_ref.shape[0] // rows
    kept = (parts - cut) * rows
    for copy in copies[len(chunks) :]:
        copy.wait()
    cots = cots_ref[...].astype(F32)
    real, imag = packed_tiles(wave_dev, index, cots, values_ref, table_ref)
    second_ref[pl.ds(kept, real.shape[0]), :] = jnp.where(core == 0, real, imag)
    send_ref[pl.ds(spec_rows, real.shape[0]), :] = jnp.where(core == 0, imag, real).astype(BF16)

    for copy in copies[: len(chunks)]:
        copy.wait()
    for slot, (k, first) in enumerate(chunks):
        grid = grid_ref[slot].astype(F32).reshape(width, channels).astype(BF16)
        sums = jnp.dot(wave_hi, grid, preferred_element_type=F32)
        sums = sums + jnp.dot(wave_lo, grid, preferred_element_type=F32)
        total_ref[k, :, pl.ds(first, TILE), :] = sums.reshape(parts, TILE, channels)
    send_ref[pl.ds(0, spec_rows), :] = total_ref[0].reshape(spec_rows, channels).astype(BF16)
    kept_total = total_ref[1].reshape(spec_rows, channels)
    first_ref[...] = kept_total[: cut * rows]
    second_ref[pl.ds(0, kept), :] = kept_total[cut * rows :]


def legendre_kernel(
    rows, first_ref, first_got_ref, second_ref, second_got_ref, out_ref
):
    degrees = TILE
    groups = degrees // 2 + 1
    first = first_ref[...] + first_got_ref[...].astype(F32)
    second = second_ref[...] + second_got_ref[...].astype(F32)
    spec_rows = 2 * degrees * rows
    spec = jnp.concatenate([first, second], axis=0)
    packed = groups * 2 * degrees
    table = spec[spec_rows + packed :]
    coefs = []
    for part in range(2):
        for group in range(groups):
            at, lane = group // 2 * degrees, group % 2 * LANES
            basis = table[at : at + degrees, lane : lane + LANES]
            basis = basis[:, : 2 * rows] + basis[:, 2 * rows : 4 * rows]
            partner = degrees - group if 0 < group < degrees - group else group
            low = (2 * group + part) * rows
            high = (2 * partner + part) * rows
            block = jnp.concatenate([spec[low : low + rows], spec[high : high + rows]], axis=0)
            coefs.append(
                jnp.dot(basis, block, preferred_element_type=F32, precision=lax.Precision.HIGHEST)
            )
    coefs.append(spec[spec_rows : spec_rows + packed])
    out_ref[...] = jnp.concatenate(coefs, axis=0).astype(BF16)


def mixing_kernel(
    wave_dev, samples, where_ref, mine_ref, other_ref, mixing_ref, mixed_ref, grad_ref, cot_ref, out_ref
):
    degrees, channels = mixing_ref.shape[:2]
    groups = degrees // 2 + 1
    slots = groups * degrees
    terms = 2 * samples * slots
    index = where_ref[0]
    core = lax.rem(index, 2)
    mine, other = mine_ref[...].astype(F32), other_ref[...].astype(F32)
    held = [jnp.where(core == k, mine, other) for k in range(2)]
    coef = [held[sample][part * slots : (part + 1) * slots] for part in range(2) for sample in range(2)]
    coef = jnp.concatenate(coef, axis=0).astype(BF16)
    cots = []
    for part in range(2):
        packed = held[part][2 * slots :]
        for lane in range(2):
            half = packed[:, lane * LANES : (lane + 1) * LANES]
            cot_ref[part, pl.ds(lane * packed.shape[0], packed.shape[0]), :] = half
        for sample in range(samples):
            halves = [
                cot_ref[part, pl.ds(2 * lane + sample, slots, stride=2 * samples), :]
                for lane in range(2)
            ]
            cots.append(jnp.concatenate(halves, axis=1))
    cot = jnp.concatenate(cots, axis=0).astype(BF16)

    block = 2 * TILE
    shape = (block, terms)
    row = lax.broadcasted_iota(jnp.int32, shape, 0)
    term = lax.broadcasted_iota(jnp.int32, shape, 1)
    wave = index * wave_dev + row // 2
    tile = jnp.where(wave < groups, wave * degrees, (degrees - wave) * degrees - wave)
    base = row % 2 * (samples * slots) + tile
    chosen = []
    for degree in range(degrees):
        for sample in range(samples):
            hit = jnp.where(wave <= degree, base + (sample * slots + degree), -1)
            chosen.append(jnp.where(term == hit, 1.0, 0.0).astype(BF16))
    chosen = jnp.concatenate(chosen, axis=0)
    lhs = jnp.dot(chosen, coef, preferred_element_type=F32).astype(BF16)
    count = 2 * wave_dev
    for degree in range(degrees):
        at = degree * samples * block
        mixed = jnp.dot(
            lhs[at : at + samples * block], mixing_ref[degree], preferred_element_type=F32
        )
        for sample in range(samples):
            for lane in range(2):
                part = mixed[sample * block : sample * block + count, lane * LANES : (lane + 1) * LANES]
                at = degree * 2 * samples * count + 2 * lane + sample
                out_ref[pl.ds(at, count, stride=2 * samples), :] = part
    mixed_ref[...] = out_ref[...].astype(BF16)

    own = grad_ref.shape[0]
    channel = lax.broadcasted_iota(jnp.int32, (own, channels), 1)
    row = lax.broadcasted_iota(jnp.int32, (own, channels), 0)
    pick = jnp.where(channel == index * own + row, 1.0, 0.0).astype(BF16)
    turned = lax.dot_general(
        pick, coef, (((1,), (1,)), ((), ())), preferred_element_type=F32
    )
    shape = (degrees, terms)
    slot = lax.broadcasted_iota(jnp.int32, shape, 1) % slots
    place, group = slot % degrees, slot // degrees
    degree = jnp.where(place >= group, place, place + degrees - group)
    of_degree = degree == lax.broadcasted_iota(jnp.int32, shape, 0)
    turned = [jnp.where(of_degree, turned[k : k + 1], 0.0) for k in range(own)]
    turned = jnp.concatenate(turned, axis=0).astype(BF16)
    grad = jnp.dot(turned, cot, preferred_element_type=F32)
    grad_ref[...] = grad.reshape(own, degrees, channels)


def sparse_shards(fields, legendre, mixing, cotangent):
    samples, rows, cells, channels = fields.shape
    lon_count = lax.axis_size("lon")
    wave_dev, degrees = legendre.shape[1:]
    parts = 2 * degrees
    spec_rows = parts * rows
    packed_rows = (degrees // 2 + 1) * parts
    index = lax.axis_index("lon")
    where = index.reshape(1).astype(jnp.int32)
    whole = pl.BlockSpec(memory_space=pltpu.VMEM)
    scalar = pl.BlockSpec(memory_space=pltpu.SMEM)
    params = pltpu.CompilerParams(vmem_limit_bytes=VMEM_BYTES)

    def in_hbm(array):
        return pltpu.with_memory_space_constraint(array, pltpu.HBM)

    def exchange(array, even, odd):
        pairs = [(i, i ^ (odd if i % 2 else even)) for i in range(lon_count)]
        return lax.ppermute(array, "lon", pairs)

    cut = (parts // 2 + 2) * rows
    rest = spec_rows - cut + packed_rows + (degrees // 4 + 1) * TILE
    halves = cotangent.reshape(degrees, wave_dev, 2, samples, 2, LANES)
    halves = halves.transpose(0, 1, 2, 4, 3, 5).reshape(-1, LANES)
    chunks = samples * rows // TILE
    far = pl.BlockSpec(memory_space=pltpu.HBM)
    acc_a, acc_b, send = pl.pallas_call(
        functools.partial(fourier_kernel, cells * lon_count),
        out_shape=(
            jax.ShapeDtypeStruct((cut, channels), F32),
            jax.ShapeDtypeStruct((rest, channels), F32),
            jax.ShapeDtypeStruct((cut + rest, channels), BF16),
        ),
        in_specs=[scalar, far, far, far],
        out_specs=(whole, whole, whole),
        scratch_shapes=[
            pltpu.VMEM((chunks, TILE, cells, channels), BF16),
            pltpu.VMEM((wave_dev, degrees, rows), F32),
            pltpu.VMEM(halves.shape, BF16),
            pltpu.VMEM((2, parts, rows, channels), F32),
            pltpu.VMEM((wave_dev, degrees, LANES), F32),
            pltpu.SemaphoreType.DMA((chunks + 2,)),
        ],
        compiler_params=params,
    )(where, in_hbm(fields), in_hbm(legendre.transpose(1, 2, 0)), in_hbm(halves))

    got = exchange(send, 1, 1)
    acc_a = acc_a + got[:cut].astype(F32)
    acc_b = acc_b + got[cut:].astype(F32)
    orders_a, orders_b = hop_orders(lon_count)
    for step, (hops_a, hops_b) in enumerate(zip(orders_a, orders_b)):
        got_a = exchange(acc_a.astype(BF16), *hops_a)
        got_b = exchange(acc_b.astype(BF16), *hops_b)
        if step < len(orders_a) - 1:
            acc_a = acc_a + got_a.astype(F32)
            acc_b = acc_b + got_b.astype(F32)

    mine = pl.pallas_call(
        functools.partial(legendre_kernel, rows),
        out_shape=jax.ShapeDtypeStruct((2 * packed_rows, channels), BF16),
        in_specs=[whole] * 4,
        out_specs=whole,
        compiler_params=params,
    )(acc_a, got_a, acc_b, got_b)
    other = exchange(mine, 1, 1)

    block_rows = 2 * wave_dev * samples
    mixed, grad = pl.pallas_call(
        functools.partial(mixing_kernel, wave_dev, samples),
        out_shape=(
            jax.ShapeDtypeStruct((degrees * block_rows * 2, LANES), BF16),
            jax.ShapeDtypeStruct((channels // lon_count, degrees, channels), F32),
        ),
        in_specs=[scalar] + [whole] * 3,
        out_specs=(whole, whole),
        scratch_shapes=[
            pltpu.VMEM((2, packed_rows * 2, LANES), F32),
            pltpu.VMEM((degrees * block_rows * 2, LANES), F32),
        ],
        compiler_params=params,
    )(where, mine, other, mixing)
    mixed = mixed.reshape(degrees, wave_dev, 2, 2, samples, LANES).transpose(0, 1, 2, 4, 3, 5)
    return mixed.reshape(degrees, wave_dev, 2, samples, channels), grad


def hop_orders(lon_count):
    bits = [1 << k for k in range(1, lon_count.bit_length() - 1)]
    bits[-1] += bits[-2]
    half = len(bits) // 2
    near, far = bits[:half], bits[half:]
    chain_a = list(zip(near + far, far + near))
    chain_b = list(zip(near[::-1] + far[::-1], far[::-1] + near[::-1]))
    return chain_a, chain_b


def few_waves(mesh, fields, legendre):
    samples, rows, longitudes, channels = fields.shape
    waves, degrees = legendre.shape[1:]
    count = mesh.shape["lon"]
    return (
        mesh.shape["lat"] == 1
        and samples == 2
        and count >= 8
        and count & (count - 1) == 0
        and degrees == TILE
        and degrees <= waves
        and rows % TILE == 0
        and 4 * rows <= LANES
        and channels == 2 * LANES
        and channels // count == TILE
        and longitudes % 4 == 0
        and (4 * waves // count) % TILE == 0
    )


def solution(mesh):
    placed = (
        P(None, "lat", "lon", None),
        P("lat", "lon", None),
        P("lat", None, None),
        P("lat", "lon", None, None, None),
    )

    def program(fields, legendre, mixing, cotangent):
        body = sparse_shards if few_waves(mesh, fields, legendre) else dense_shards
        return jax.shard_map(
            body,
            mesh=mesh,
            in_specs=placed,
            out_specs=(P("lat", "lon", None, None, None), P("lon", "lat", None)),
            check_vma=False,
        )(fields, legendre, mixing, cotangent)

    return program
```

```python
import functools
import math

import jax
import jax.numpy as jnp
from jax import lax
from jax.experimental import pallas as pl
from jax.experimental.pallas import tpu as pltpu
from jax.sharding import PartitionSpec as P

F32 = jnp.float32
BF16 = jnp.bfloat16
TILE = 8
LANES = 128
VMEM_BYTES = 32 * 1024 * 1024


def dense_shards(fields, legendre, mixing, cotangent):
    samples = fields.shape[0]
    lat_rows = fields.shape[1]
    lon_cells = fields.shape[2]
    channels = fields.shape[3]
    lon_count = lax.axis_size("lon")
    lat_count = lax.axis_size("lat")
    nlon_total = lon_cells * lon_count
    wave_dev = legendre.shape[1]
    wave_total = wave_dev * lon_count
    degrees = legendre.shape[2]
    degree_dev = degrees // lat_count
    column_rows = 2 * wave_dev * samples
    column_width = 2 * samples * channels
    positions = jnp.arange(nlon_total, dtype=jnp.int32)
    wavenums = jnp.arange(wave_total, dtype=jnp.int32)
    phase = (positions[:, None] * wavenums[None, :] % nlon_total).astype(jnp.float32) * (
        2.0 * math.pi / nlon_total
    )
    fourier = jnp.stack([jnp.cos(phase), -jnp.sin(phase)], axis=2).reshape(
        nlon_total, 2 * wave_total
    )
    fourier = fourier * (1.0 / nlon_total**0.5)
    fourier_hi = fourier.astype(jnp.bfloat16)
    fourier_lo = (fourier - fourier_hi.astype(jnp.float32)).astype(jnp.bfloat16)
    portion = lax.all_to_all(fields, "lon", split_axis=3, concat_axis=2, tiled=True)
    spectrum = jnp.einsum("bjkc,kf->jfbc", portion, fourier_hi, preferred_element_type=jnp.float32)
    spectrum = spectrum + jnp.einsum(
        "bjkc,kf->jfbc", portion, fourier_lo, preferred_element_type=jnp.float32
    )
    owned = lax.all_to_all(spectrum, "lon", split_axis=1, concat_axis=3, tiled=True)
    spectral = owned.reshape(owned.shape[0], column_rows, channels)
    wave_global = lax.axis_index("lon") * wave_dev + jnp.arange(wave_dev, dtype=jnp.int32)
    degree_ids = jnp.arange(degrees, dtype=jnp.int32)
    keep = degree_ids[None, None, :] >= wave_global[None, :, None]
    basis = jnp.where(keep, legendre, jnp.float32(0.0))
    spectral_waves = spectral.reshape(lat_rows, wave_dev, column_width)
    summed = lax.psum_scatter(
        jnp.einsum("jml,jmq->lmq", basis, spectral_waves, precision=lax.Precision.HIGHEST),
        "lat",
        scatter_dimension=0,
        tiled=True,
    )
    coef = summed.reshape(degree_dev, column_rows, channels)
    coef_bf = coef.astype(jnp.bfloat16)
    mixed = jnp.einsum("lrc,lcd->lrd", coef_bf, mixing, preferred_element_type=jnp.float32)
    mixed = mixed.astype(jnp.bfloat16).reshape(degree_dev, wave_dev, 2, samples, channels)
    cot_rows = cotangent.reshape(degree_dev, column_rows, channels)
    weight_grad = lax.psum_scatter(
        jnp.einsum("lrc,lrd->cld", coef_bf, cot_rows, preferred_element_type=jnp.float32),
        "lon",
        scatter_dimension=0,
        tiled=True,
    )
    return (mixed, weight_grad)


def tile_slots(degrees):
    slots = []
    for group in range(degrees // 2 + 1):
        for place in range(degrees):
            if place >= group:
                slots.append((group, place))
            elif group < degrees - group:
                slots.append((degrees - group, place + degrees - group))
            else:
                slots.append(None)
    return slots


def packed_tiles(wave_dev, index, cots, legendre_ref, table_ref):
    degrees, rows = legendre_ref.shape[1:]
    slots = tile_slots(degrees)
    row = lax.broadcasted_iota(jnp.int32, (TILE, LANES), 0)
    zeros = jnp.zeros((TILE, LANES), F32)
    owned = [index == owner for owner in range((degrees - 1) // wave_dev + 1)]

    def cotangent(slot):
        if slot is None:
            return zeros
        wave, degree = slot
        at = (degree * wave_dev + wave % wave_dev) * TILE
        return jnp.where(owned[wave // wave_dev], cots[at : at + TILE], 0.0)

    upper = row < TILE // 2
    parts = ([], [])
    for pair in range(len(slots) // 2):
        one, two = cotangent(slots[2 * pair]), cotangent(slots[2 * pair + 1])
        parts[0].append(jnp.where(upper, one, pltpu.roll(two, TILE // 2, 0)))
        parts[1].append(jnp.where(upper, pltpu.roll(one, TILE // 2, 0), two))

    table_ref[...] = jnp.zeros(table_ref.shape, F32)
    table_ref[:, :, pl.ds(0, rows)] = legendre_ref[...]

    def basis(wave):
        block = jnp.where(owned[wave // wave_dev], table_ref[wave % wave_dev], 0.0)
        return jnp.where(row >= wave, block, 0.0)

    table = jnp.zeros((degrees, 2 * LANES), F32)
    for group in range(degrees // 2 + 1):
        block = basis(group)
        if 0 < group < degrees - group:
            rest = pltpu.roll(basis(degrees - group), group, 0)
            block = block + pltpu.roll(rest, rows, 1)
        block = jnp.concatenate([block, zeros], axis=1)
        table = table + (pltpu.roll(block, 2 * rows * group, 1) if group else block)
    high = table.astype(BF16).astype(F32)

    half = len(slots) // 4
    whole = []
    for tiles in parts:
        lanes = [tiles[lane * half : (lane + 1) * half] for lane in range(2)]
        cots = jnp.concatenate([jnp.concatenate(lane, axis=0) for lane in lanes], axis=1)
        whole.append(jnp.concatenate([cots, high, table - high], axis=0))
    return whole


def fourier_kernel(
    nlon_total,
    where_ref,
    fields_ref,
    legendre_ref,
    cot_ref,
    first_ref,
    second_ref,
    first_send_ref,
    second_send_ref,
    grid_ref,
    values_ref,
    cots_ref,
    total_ref,
    table_ref,
    sems,
):
    rows, cells, channels = fields_ref.shape[1:]
    wave_dev, degrees = legendre_ref.shape[:2]
    parts = 2 * degrees
    spec_rows = parts * rows
    index = where_ref[0]
    core = lax.rem(index, 2)
    chunks = [(k, first) for k in range(2) for first in range(0, rows, TILE)]
    copies = []
    for slot, (k, first) in enumerate(chunks):
        sample = 1 - core if k == 0 else core
        copies.append(
            pltpu.make_async_copy(
                fields_ref.at[sample, pl.ds(first, TILE)], grid_ref.at[slot], sems.at[slot]
            )
        )
    copies.append(pltpu.make_async_copy(legendre_ref, values_ref, sems.at[len(chunks)]))
    copies.append(pltpu.make_async_copy(cot_ref, cots_ref, sems.at[len(chunks) + 1]))
    for copy in copies:
        copy.start()
    width = TILE * cells
    column = lax.broadcasted_iota(jnp.int32, (parts, width), 1)
    part = lax.broadcasted_iota(jnp.int32, (parts, width), 0)
    cell = index * cells + lax.rem(column, cells)
    turn = lax.rem(cell * (part // 2) + lax.rem(part, 2) * (nlon_total // 4), nlon_total)
    wave = jnp.cos(turn.astype(F32) * (2.0 * math.pi / nlon_total)) * (1.0 / nlon_total**0.5)
    spread = (parts, TILE, width)
    own_row = (
        lax.broadcasted_iota(jnp.int32, spread, 2) // cells
        == lax.broadcasted_iota(jnp.int32, spread, 1)
    )
    wave = jnp.where(own_row, jnp.broadcast_to(wave[:, None, :], spread), 0.0)
    wave = wave.reshape(parts * TILE, width)
    wave_hi = wave.astype(BF16)
    wave_lo = (wave - wave_hi.astype(F32)).astype(BF16)
    cut = first_ref.shape[0] // rows
    kept = (parts - cut) * rows
    for copy in copies[len(chunks) :]:
        copy.wait()
    cots = cots_ref[...].astype(F32)
    real, imag = packed_tiles(wave_dev, index, cots, values_ref, table_ref)
    second_ref[pl.ds(kept, real.shape[0]), :] = jnp.where(core == 0, real, imag)
    second_send_ref[pl.ds(kept, real.shape[0]), :] = jnp.where(core == 0, imag, real).astype(BF16)

    for copy in copies[: len(chunks)]:
        copy.wait()
    for slot, (k, first) in enumerate(chunks):
        grid = grid_ref[slot].astype(F32).reshape(width, channels).astype(BF16)
        sums = jnp.dot(wave_hi, grid, preferred_element_type=F32)
        sums = sums + jnp.dot(wave_lo, grid, preferred_element_type=F32)
        for part in range(parts):
            tile = sums[part * TILE : (part + 1) * TILE]
            if k == 0:
                total_ref[pl.ds(part * rows + first, TILE), :] = tile
            elif part < cut:
                first_ref[pl.ds(part * rows + first, TILE), :] = tile
            else:
                second_ref[pl.ds((part - cut) * rows + first, TILE), :] = tile
        if k == 0 and first + TILE == rows:
            first_send_ref[...] = total_ref[pl.ds(0, cut * rows), :].astype(BF16)
            second_send_ref[pl.ds(0, kept), :] = total_ref[pl.ds(cut * rows, kept), :].astype(BF16)


def legendre_kernel(
    rows, first_ref, first_got_ref, second_ref, second_got_ref, out_ref
):
    degrees = TILE
    groups = degrees // 2 + 1
    first = first_ref[...] + first_got_ref[...].astype(F32)
    second = second_ref[...] + second_got_ref[...].astype(F32)
    spec_rows = 2 * degrees * rows
    spec = jnp.concatenate([first, second], axis=0)
    packed = groups * 2 * degrees
    table = spec[spec_rows + packed :]
    spec_hi = spec[:spec_rows].astype(BF16).astype(F32)
    spec_lo = spec[:spec_rows] - spec_hi
    coefs = []
    for part in range(2):
        for group in range(groups):
            basis = table[:, 2 * rows * group : 2 * rows * (group + 1)].astype(BF16)
            partner = degrees - group if 0 < group < degrees - group else group
            low = (2 * group + part) * rows
            high = (2 * partner + part) * rows
            block, rest = (
                jnp.concatenate([half[low : low + rows], half[high : high + rows]], axis=0)
                for half in (spec_hi, spec_lo)
            )
            sums = jnp.dot(basis, block.astype(BF16), preferred_element_type=F32)
            more = jnp.dot(basis[:degrees], rest.astype(BF16), preferred_element_type=F32)
            coefs.append(sums[:degrees] + sums[degrees:] + more)
    coefs.append(spec[spec_rows : spec_rows + packed])
    out_ref[...] = jnp.concatenate(coefs, axis=0).astype(BF16)


def mixing_kernel(
    wave_dev, samples, where_ref, mine_ref, other_ref, mixing_ref, mixed_ref, grad_ref, cot_ref, out_ref
):
    degrees, channels = mixing_ref.shape[:2]
    groups = degrees // 2 + 1
    slots = groups * degrees
    terms = 2 * samples * slots
    index = where_ref[0]
    core = lax.rem(index, 2)
    mine, other = mine_ref[...].astype(F32), other_ref[...].astype(F32)
    held = [jnp.where(core == k, mine, other) for k in range(2)]
    coef = [held[sample][part * slots : (part + 1) * slots] for part in range(2) for sample in range(2)]
    coef = jnp.concatenate(coef, axis=0).astype(BF16)
    cots = []
    for part in range(2):
        packed = held[part][2 * slots :]
        for lane in range(2):
            half = packed[:, lane * LANES : (lane + 1) * LANES]
            cot_ref[part, pl.ds(lane * packed.shape[0], packed.shape[0]), :] = half
        for sample in range(samples):
            halves = [
                cot_ref[part, pl.ds(2 * lane + sample, slots, stride=2 * samples), :]
                for lane in range(2)
            ]
            cots.append(jnp.concatenate(halves, axis=1))
    cot = jnp.concatenate(cots, axis=0).astype(BF16)

    block = 2 * TILE
    shape = (block, terms)
    row = lax.broadcasted_iota(jnp.int32, shape, 0)
    term = lax.broadcasted_iota(jnp.int32, shape, 1)
    wave = index * wave_dev + row // 2
    tile = jnp.where(wave < groups, wave * degrees, (degrees - wave) * degrees - wave)
    base = row % 2 * (samples * slots) + tile
    chosen = []
    for degree in range(degrees):
        for sample in range(samples):
            hit = jnp.where(wave <= degree, base + (sample * slots + degree), -1)
            chosen.append(jnp.where(term == hit, 1.0, 0.0).astype(BF16))
    chosen = jnp.concatenate(chosen, axis=0)
    lhs = jnp.dot(chosen, coef, preferred_element_type=F32).astype(BF16)
    count = 2 * wave_dev
    for degree in range(degrees):
        at = degree * samples * block
        mixed = jnp.dot(
            lhs[at : at + samples * block], mixing_ref[degree], preferred_element_type=F32
        )
        for sample in range(samples):
            for lane in range(2):
                part = mixed[sample * block : sample * block + count, lane * LANES : (lane + 1) * LANES]
                at = degree * 2 * samples * count + 2 * lane + sample
                out_ref[pl.ds(at, count, stride=2 * samples), :] = part
    mixed_ref[...] = out_ref[...].astype(BF16)

    own = grad_ref.shape[0]
    channel = lax.broadcasted_iota(jnp.int32, (own, channels), 1)
    row = lax.broadcasted_iota(jnp.int32, (own, channels), 0)
    pick = jnp.where(channel == index * own + row, 1.0, 0.0).astype(BF16)
    turned = lax.dot_general(
        pick, coef, (((1,), (1,)), ((), ())), preferred_element_type=F32
    )
    shape = (degrees, terms)
    slot = lax.broadcasted_iota(jnp.int32, shape, 1) % slots
    place, group = slot % degrees, slot // degrees
    degree = jnp.where(place >= group, place, place + degrees - group)
    of_degree = degree == lax.broadcasted_iota(jnp.int32, shape, 0)
    turned = [jnp.where(of_degree, turned[k : k + 1], 0.0) for k in range(own)]
    turned = jnp.concatenate(turned, axis=0).astype(BF16)
    grad = jnp.dot(turned, cot, preferred_element_type=F32)
    grad_ref[...] = grad.reshape(own, degrees, channels)


def sparse_shards(fields, legendre, mixing, cotangent):
    samples, rows, cells, channels = fields.shape
    lon_count = lax.axis_size("lon")
    wave_dev, degrees = legendre.shape[1:]
    parts = 2 * degrees
    spec_rows = parts * rows
    packed_rows = (degrees // 2 + 1) * parts
    index = lax.axis_index("lon")
    where = index.reshape(1).astype(jnp.int32)
    whole = pl.BlockSpec(memory_space=pltpu.VMEM)
    scalar = pl.BlockSpec(memory_space=pltpu.SMEM)
    params = pltpu.CompilerParams(vmem_limit_bytes=VMEM_BYTES)

    def in_hbm(array):
        return pltpu.with_memory_space_constraint(array, pltpu.HBM)

    def exchange(array, even, odd):
        pairs = [(i, i ^ (odd if i % 2 else even)) for i in range(lon_count)]
        return lax.ppermute(array, "lon", pairs)

    cut = (parts // 2 + 2) * rows
    rest = spec_rows - cut + packed_rows + 2 * TILE
    halves = cotangent.reshape(degrees, wave_dev, 2, samples, 2, LANES)
    halves = halves.transpose(0, 1, 2, 4, 3, 5).reshape(-1, LANES)
    chunks = samples * rows // TILE
    far = pl.BlockSpec(memory_space=pltpu.HBM)
    acc_a, acc_b, send_a, send_b = pl.pallas_call(
        functools.partial(fourier_kernel, cells * lon_count),
        out_shape=(
            jax.ShapeDtypeStruct((cut, channels), F32),
            jax.ShapeDtypeStruct((rest, channels), F32),
            jax.ShapeDtypeStruct((cut, channels), BF16),
            jax.ShapeDtypeStruct((rest, channels), BF16),
        ),
        in_specs=[scalar, far, far, far],
        out_specs=(whole, whole, whole, whole),
        scratch_shapes=[
            pltpu.VMEM((chunks, TILE, cells, channels), BF16),
            pltpu.VMEM((wave_dev, degrees, rows), F32),
            pltpu.VMEM(halves.shape, BF16),
            pltpu.VMEM((spec_rows, channels), F32),
            pltpu.VMEM((wave_dev, degrees, LANES), F32),
            pltpu.SemaphoreType.DMA((chunks + 2,)),
        ],
        compiler_params=params,
    )(where, in_hbm(fields), in_hbm(legendre.transpose(1, 2, 0)), in_hbm(halves))

    acc_a = acc_a + exchange(send_a, 1, 1).astype(F32)
    acc_b = acc_b + exchange(send_b, 1, 1).astype(F32)
    orders_a, orders_b = hop_orders(lon_count)
    for step, (hops_a, hops_b) in enumerate(zip(orders_a, orders_b)):
        got_a = exchange(acc_a.astype(BF16), *hops_a)
        got_b = exchange(acc_b.astype(BF16), *hops_b)
        if step < len(orders_a) - 1:
            acc_a = acc_a + got_a.astype(F32)
            acc_b = acc_b + got_b.astype(F32)

    mine = pl.pallas_call(
        functools.partial(legendre_kernel, rows),
        out_shape=jax.ShapeDtypeStruct((2 * packed_rows, channels), BF16),
        in_specs=[whole] * 4,
        out_specs=whole,
        compiler_params=params,
    )(acc_a, got_a, acc_b, got_b)
    other = exchange(mine, 1, 1)

    block_rows = 2 * wave_dev * samples
    mixed, grad = pl.pallas_call(
        functools.partial(mixing_kernel, wave_dev, samples),
        out_shape=(
            jax.ShapeDtypeStruct((degrees * block_rows * 2, LANES), BF16),
            jax.ShapeDtypeStruct((channels // lon_count, degrees, channels), F32),
        ),
        in_specs=[scalar] + [whole] * 3,
        out_specs=(whole, whole),
        scratch_shapes=[
            pltpu.VMEM((2, packed_rows * 2, LANES), F32),
            pltpu.VMEM((degrees * block_rows * 2, LANES), F32),
        ],
        compiler_params=params,
    )(where, mine, other, mixing)
    mixed = mixed.reshape(degrees, wave_dev, 2, 2, samples, LANES).transpose(0, 1, 2, 4, 3, 5)
    return mixed.reshape(degrees, wave_dev, 2, samples, channels), grad


def hop_orders(lon_count):
    bits = [1 << k for k in range(1, lon_count.bit_length() - 1)]
    bits[-1] += bits[-2]
    half = len(bits) // 2
    near, far = bits[:half], bits[half:]
    chain_a = list(zip(near + far, far + near))
    chain_b = list(zip(near[::-1] + far[::-1], far[::-1] + near[::-1]))
    return chain_a, chain_b


def few_waves(mesh, fields, legendre):
    samples, rows, longitudes, channels = fields.shape
    waves, degrees = legendre.shape[1:]
    count = mesh.shape["lon"]
    return (
        mesh.shape["lat"] == 1
        and samples == 2
        and count >= 8
        and count & (count - 1) == 0
        and degrees == TILE
        and degrees <= waves
        and rows % TILE == 0
        and 2 * rows * (degrees // 2 + 1) <= channels
        and channels == 2 * LANES
        and channels // count == TILE
        and longitudes % 4 == 0
        and (4 * waves // count) % TILE == 0
    )


def solution(mesh):
    placed = (
        P(None, "lat", "lon", None),
        P("lat", "lon", None),
        P("lat", None, None),
        P("lat", "lon", None, None, None),
    )

    def program(fields, legendre, mixing, cotangent):
        body = sparse_shards if few_waves(mesh, fields, legendre) else dense_shards
        return jax.shard_map(
            body,
            mesh=mesh,
            in_specs=placed,
            out_specs=(P("lat", "lon", None, None, None), P("lon", "lat", None)),
            check_vma=False,
        )(fields, legendre, mixing, cotangent)

    return program
```

```python
import functools
import math

import jax
import jax.numpy as jnp
from jax import lax
from jax.experimental import pallas as pl
from jax.experimental.pallas import tpu as pltpu
from jax.sharding import PartitionSpec as P

F32 = jnp.float32
BF16 = jnp.bfloat16
TILE = 8
LANES = 128
VMEM_BYTES = 32 * 1024 * 1024


def dense_shards(fields, legendre, mixing, cotangent):
    samples = fields.shape[0]
    lat_rows = fields.shape[1]
    lon_cells = fields.shape[2]
    channels = fields.shape[3]
    lon_count = lax.axis_size("lon")
    lat_count = lax.axis_size("lat")
    nlon_total = lon_cells * lon_count
    wave_dev = legendre.shape[1]
    wave_total = wave_dev * lon_count
    degrees = legendre.shape[2]
    degree_dev = degrees // lat_count
    column_rows = 2 * wave_dev * samples
    column_width = 2 * samples * channels
    positions = jnp.arange(nlon_total, dtype=jnp.int32)
    wavenums = jnp.arange(wave_total, dtype=jnp.int32)
    phase = (positions[:, None] * wavenums[None, :] % nlon_total).astype(jnp.float32) * (
        2.0 * math.pi / nlon_total
    )
    fourier = jnp.stack([jnp.cos(phase), -jnp.sin(phase)], axis=2).reshape(
        nlon_total, 2 * wave_total
    )
    fourier = fourier * (1.0 / nlon_total**0.5)
    fourier_hi = fourier.astype(jnp.bfloat16)
    fourier_lo = (fourier - fourier_hi.astype(jnp.float32)).astype(jnp.bfloat16)
    portion = lax.all_to_all(fields, "lon", split_axis=3, concat_axis=2, tiled=True)
    spectrum = jnp.einsum("bjkc,kf->jfbc", portion, fourier_hi, preferred_element_type=jnp.float32)
    spectrum = spectrum + jnp.einsum(
        "bjkc,kf->jfbc", portion, fourier_lo, preferred_element_type=jnp.float32
    )
    owned = lax.all_to_all(spectrum, "lon", split_axis=1, concat_axis=3, tiled=True)
    spectral = owned.reshape(owned.shape[0], column_rows, channels)
    wave_global = lax.axis_index("lon") * wave_dev + jnp.arange(wave_dev, dtype=jnp.int32)
    degree_ids = jnp.arange(degrees, dtype=jnp.int32)
    keep = degree_ids[None, None, :] >= wave_global[None, :, None]
    basis = jnp.where(keep, legendre, jnp.float32(0.0))
    spectral_waves = spectral.reshape(lat_rows, wave_dev, column_width)
    summed = lax.psum_scatter(
        jnp.einsum("jml,jmq->lmq", basis, spectral_waves, precision=lax.Precision.HIGHEST),
        "lat",
        scatter_dimension=0,
        tiled=True,
    )
    coef = summed.reshape(degree_dev, column_rows, channels)
    coef_bf = coef.astype(jnp.bfloat16)
    mixed = jnp.einsum("lrc,lcd->lrd", coef_bf, mixing, preferred_element_type=jnp.float32)
    mixed = mixed.astype(jnp.bfloat16).reshape(degree_dev, wave_dev, 2, samples, channels)
    cot_rows = cotangent.reshape(degree_dev, column_rows, channels)
    weight_grad = lax.psum_scatter(
        jnp.einsum("lrc,lrd->cld", coef_bf, cot_rows, preferred_element_type=jnp.float32),
        "lon",
        scatter_dimension=0,
        tiled=True,
    )
    return (mixed, weight_grad)


def tile_slots(degrees):
    slots = []
    for group in range(degrees // 2 + 1):
        for place in range(degrees):
            if place >= group:
                slots.append((group, place))
            elif group < degrees - group:
                slots.append((degrees - group, place + degrees - group))
            else:
                slots.append(None)
    return slots


def packed_tiles(wave_dev, index, cots, legendre_ref, table_ref):
    degrees, rows = legendre_ref.shape[1:]
    slots = tile_slots(degrees)
    row = lax.broadcasted_iota(jnp.int32, (TILE, LANES), 0)
    zeros = jnp.zeros((TILE, LANES), F32)
    owned = [index == owner for owner in range((degrees - 1) // wave_dev + 1)]

    def cotangent(slot):
        if slot is None:
            return zeros
        wave, degree = slot
        at = (degree * wave_dev + wave % wave_dev) * TILE
        return jnp.where(owned[wave // wave_dev], cots[at : at + TILE], 0.0)

    upper = row < TILE // 2
    parts = ([], [])
    for pair in range(len(slots) // 2):
        one, two = cotangent(slots[2 * pair]), cotangent(slots[2 * pair + 1])
        parts[0].append(jnp.where(upper, one, pltpu.roll(two, TILE // 2, 0)))
        parts[1].append(jnp.where(upper, pltpu.roll(one, TILE // 2, 0), two))

    table_ref[...] = jnp.zeros(table_ref.shape, F32)
    table_ref[:, :, pl.ds(0, rows)] = legendre_ref[...]

    def basis(wave):
        block = jnp.where(owned[wave // wave_dev], table_ref[wave % wave_dev], 0.0)
        return jnp.where(row >= wave, block, 0.0)

    table = jnp.zeros((degrees, 2 * LANES), F32)
    for group in range(degrees // 2 + 1):
        block = basis(group)
        if 0 < group < degrees - group:
            rest = pltpu.roll(basis(degrees - group), group, 0)
            block = block + pltpu.roll(rest, rows, 1)
        block = jnp.concatenate([block, zeros], axis=1)
        table = table + (pltpu.roll(block, 2 * rows * group, 1) if group else block)
    high = table.astype(BF16).astype(F32)

    half = len(slots) // 4
    whole = []
    for tiles in parts:
        lanes = [tiles[lane * half : (lane + 1) * half] for lane in range(2)]
        cots = jnp.concatenate([jnp.concatenate(lane, axis=0) for lane in lanes], axis=1)
        whole.append(jnp.concatenate([cots, high, table - high], axis=0))
    return whole


def side_of(index, lon_count):
    side = index
    for bit in range(1, lon_count.bit_length() - 2):
        side = side ^ (index >> bit)
    return side & 1


def fourier_kernel(
    lon_count,
    where_ref,
    fields_ref,
    legendre_ref,
    cot_ref,
    first_ref,
    second_ref,
    first_send_ref,
    second_send_ref,
    grid_ref,
    values_ref,
    cots_ref,
    total_ref,
    table_ref,
    sems,
):
    rows, cells, channels = fields_ref.shape[1:]
    wave_dev, degrees = legendre_ref.shape[:2]
    parts = 2 * degrees
    spec_rows = parts * rows
    nlon_total = cells * lon_count
    index = where_ref[0]
    side = side_of(index, lon_count)
    chunks = [(k, first) for k in range(2) for first in range(0, rows, TILE)]
    copies = []
    for slot, (k, first) in enumerate(chunks):
        sample = 1 - side if k == 0 else side
        copies.append(
            pltpu.make_async_copy(
                fields_ref.at[sample, pl.ds(first, TILE)], grid_ref.at[slot], sems.at[slot]
            )
        )
    for copy in copies:
        copy.start()
    owns = index < (degrees - 1) // wave_dev + 1
    others = [
        pltpu.make_async_copy(legendre_ref, values_ref, sems.at[len(chunks)]),
        pltpu.make_async_copy(cot_ref, cots_ref, sems.at[len(chunks) + 1]),
    ]

    @pl.when(owns)
    def _():
        for copy in others:
            copy.start()

    width = TILE * cells
    column = lax.broadcasted_iota(jnp.int32, (parts, width), 1)
    part = lax.broadcasted_iota(jnp.int32, (parts, width), 0)
    cell = index * cells + lax.rem(column, cells)
    turn = lax.rem(cell * (part // 2) + lax.rem(part, 2) * (nlon_total // 4), nlon_total)
    wave = jnp.cos(turn.astype(F32) * (2.0 * math.pi / nlon_total)) * (1.0 / nlon_total**0.5)
    spread = (parts, TILE, width)
    own_row = (
        lax.broadcasted_iota(jnp.int32, spread, 2) // cells
        == lax.broadcasted_iota(jnp.int32, spread, 1)
    )
    wave = jnp.where(own_row, jnp.broadcast_to(wave[:, None, :], spread), 0.0)
    wave = wave.reshape(parts * TILE, width)
    wave_hi = wave.astype(BF16)
    wave_lo = (wave - wave_hi.astype(F32)).astype(BF16)
    cut = first_ref.shape[0] // rows
    kept = (parts - cut) * rows
    rest = pl.ds(kept, second_ref.shape[0] - kept)

    @pl.when(owns)
    def _():
        for copy in others:
            copy.wait()
        cots = cots_ref[...].astype(F32)
        real, imag = packed_tiles(wave_dev, index, cots, values_ref, table_ref)
        second_ref[rest, :] = jnp.where(side == 0, real, imag)
        second_send_ref[rest, :] = jnp.where(side == 0, imag, real).astype(BF16)

    @pl.when(jnp.logical_not(owns))
    def _():
        second_ref[rest, :] = jnp.zeros((rest.size, channels), F32)
        second_send_ref[rest, :] = jnp.zeros((rest.size, channels), BF16)


    for copy in copies:
        copy.wait()
    for slot, (k, first) in enumerate(chunks):
        grid = grid_ref[slot].astype(F32).reshape(width, channels).astype(BF16)
        sums = jnp.dot(wave_hi, grid, preferred_element_type=F32)
        sums = sums + jnp.dot(wave_lo, grid, preferred_element_type=F32)
        for part in range(parts):
            tile = sums[part * TILE : (part + 1) * TILE]
            if k == 0:
                total_ref[pl.ds(part * rows + first, TILE), :] = tile
            elif part < cut:
                first_ref[pl.ds(part * rows + first, TILE), :] = tile
            else:
                second_ref[pl.ds((part - cut) * rows + first, TILE), :] = tile
        if k == 0 and first + TILE == rows:
            first_send_ref[...] = total_ref[pl.ds(0, cut * rows), :].astype(BF16)
            second_send_ref[pl.ds(0, kept), :] = total_ref[pl.ds(cut * rows, kept), :].astype(BF16)


def legendre_kernel(
    rows, first_ref, first_got_ref, second_ref, second_got_ref, out_ref
):
    degrees = TILE
    groups = degrees // 2 + 1
    first = first_ref[...] + first_got_ref[...].astype(F32)
    second = second_ref[...] + second_got_ref[...].astype(F32)
    spec_rows = 2 * degrees * rows
    spec = jnp.concatenate([first, second], axis=0)
    packed = groups * 2 * degrees
    table = spec[spec_rows + packed :]
    spec_hi = spec[:spec_rows].astype(BF16).astype(F32)
    spec_lo = spec[:spec_rows] - spec_hi
    coefs = []
    for part in range(2):
        for group in range(groups):
            basis = table[:, 2 * rows * group : 2 * rows * (group + 1)].astype(BF16)
            partner = degrees - group if 0 < group < degrees - group else group
            low = (2 * group + part) * rows
            high = (2 * partner + part) * rows
            block, rest = (
                jnp.concatenate([half[low : low + rows], half[high : high + rows]], axis=0)
                for half in (spec_hi, spec_lo)
            )
            sums = jnp.dot(basis, block.astype(BF16), preferred_element_type=F32)
            more = jnp.dot(basis[:degrees], rest.astype(BF16), preferred_element_type=F32)
            coefs.append(sums[:degrees] + sums[degrees:] + more)
    coefs.append(spec[spec_rows : spec_rows + packed])
    out_ref[...] = jnp.concatenate(coefs, axis=0).astype(BF16)


def mixing_kernel(
    lon_count, wave_dev, samples, where_ref, mine_ref, other_ref, mixing_ref, mixed_ref, grad_ref, cot_ref, out_ref
):
    degrees, channels = mixing_ref.shape[:2]
    groups = degrees // 2 + 1
    slots = groups * degrees
    terms = 2 * samples * slots
    index = where_ref[0]
    side = side_of(index, lon_count)
    mine, other = mine_ref[...].astype(F32), other_ref[...].astype(F32)
    held = [jnp.where(side == k, mine, other) for k in range(2)]
    coef = [held[sample][part * slots : (part + 1) * slots] for part in range(2) for sample in range(2)]
    coef = jnp.concatenate(coef, axis=0).astype(BF16)
    cots = []
    for part in range(2):
        packed = held[part][2 * slots :]
        for lane in range(2):
            half = packed[:, lane * LANES : (lane + 1) * LANES]
            cot_ref[part, pl.ds(lane * packed.shape[0], packed.shape[0]), :] = half
        for sample in range(samples):
            halves = [
                cot_ref[part, pl.ds(2 * lane + sample, slots, stride=2 * samples), :]
                for lane in range(2)
            ]
            cots.append(jnp.concatenate(halves, axis=1))
    cot = jnp.concatenate(cots, axis=0).astype(BF16)

    block = 2 * TILE
    shape = (block, terms)
    row = lax.broadcasted_iota(jnp.int32, shape, 0)
    term = lax.broadcasted_iota(jnp.int32, shape, 1)
    wave = index * wave_dev + row // 2
    tile = jnp.where(wave < groups, wave * degrees, (degrees - wave) * degrees - wave)
    base = row % 2 * (samples * slots) + tile
    chosen = []
    for degree in range(degrees):
        for sample in range(samples):
            hit = jnp.where(wave <= degree, base + (sample * slots + degree), -1)
            chosen.append(jnp.where(term == hit, 1.0, 0.0).astype(BF16))
    chosen = jnp.concatenate(chosen, axis=0)
    lhs = jnp.dot(chosen, coef, preferred_element_type=F32).astype(BF16)
    count = 2 * wave_dev
    for degree in range(degrees):
        at = degree * samples * block
        mixed = jnp.dot(
            lhs[at : at + samples * block], mixing_ref[degree], preferred_element_type=F32
        )
        for sample in range(samples):
            for lane in range(2):
                part = mixed[sample * block : sample * block + count, lane * LANES : (lane + 1) * LANES]
                at = degree * 2 * samples * count + 2 * lane + sample
                out_ref[pl.ds(at, count, stride=2 * samples), :] = part
    mixed_ref[...] = out_ref[...].astype(BF16)

    own = grad_ref.shape[0]
    channel = lax.broadcasted_iota(jnp.int32, (own, channels), 1)
    row = lax.broadcasted_iota(jnp.int32, (own, channels), 0)
    pick = jnp.where(channel == index * own + row, 1.0, 0.0).astype(BF16)
    turned = lax.dot_general(
        pick, coef, (((1,), (1,)), ((), ())), preferred_element_type=F32
    )
    shape = (degrees, terms)
    slot = lax.broadcasted_iota(jnp.int32, shape, 1) % slots
    place, group = slot % degrees, slot // degrees
    degree = jnp.where(place >= group, place, place + degrees - group)
    of_degree = degree == lax.broadcasted_iota(jnp.int32, shape, 0)
    turned = [jnp.where(of_degree, turned[k : k + 1], 0.0) for k in range(own)]
    turned = jnp.concatenate(turned, axis=0).astype(BF16)
    grad = jnp.dot(turned, cot, preferred_element_type=F32)
    grad_ref[...] = grad.reshape(own, degrees, channels)


def sparse_shards(fields, legendre, mixing, cotangent):
    samples, rows, cells, channels = fields.shape
    lon_count = lax.axis_size("lon")
    wave_dev, degrees = legendre.shape[1:]
    parts = 2 * degrees
    spec_rows = parts * rows
    packed_rows = (degrees // 2 + 1) * parts
    index = lax.axis_index("lon")
    where = index.reshape(1).astype(jnp.int32)
    whole = pl.BlockSpec(memory_space=pltpu.VMEM)
    scalar = pl.BlockSpec(memory_space=pltpu.SMEM)
    params = pltpu.CompilerParams(vmem_limit_bytes=VMEM_BYTES)

    def in_hbm(array):
        return pltpu.with_memory_space_constraint(array, pltpu.HBM)

    def exchange(array, *hops):
        pairs = [(i, i ^ hops[side_of(i, lon_count)]) for i in range(lon_count)]
        return lax.ppermute(array, "lon", pairs)

    cut = (parts // 2 + 2) * rows
    rest = spec_rows - cut + packed_rows + 2 * TILE
    halves = cotangent.reshape(degrees, wave_dev, 2, samples, 2, LANES)
    halves = halves.transpose(0, 1, 2, 4, 3, 5).reshape(-1, LANES)
    chunks = samples * rows // TILE
    far = pl.BlockSpec(memory_space=pltpu.HBM)
    acc_a, acc_b, send_a, send_b = pl.pallas_call(
        functools.partial(fourier_kernel, lon_count),
        out_shape=(
            jax.ShapeDtypeStruct((cut, channels), F32),
            jax.ShapeDtypeStruct((rest, channels), F32),
            jax.ShapeDtypeStruct((cut, channels), BF16),
            jax.ShapeDtypeStruct((rest, channels), BF16),
        ),
        in_specs=[scalar, far, far, far],
        out_specs=(whole, whole, whole, whole),
        scratch_shapes=[
            pltpu.VMEM((chunks, TILE, cells, channels), BF16),
            pltpu.VMEM((wave_dev, degrees, rows), F32),
            pltpu.VMEM(halves.shape, BF16),
            pltpu.VMEM((spec_rows, channels), F32),
            pltpu.VMEM((wave_dev, degrees, LANES), F32),
            pltpu.SemaphoreType.DMA((chunks + 2,)),
        ],
        compiler_params=params,
    )(where, in_hbm(fields), in_hbm(legendre.transpose(1, 2, 0)), in_hbm(halves))

    acc_a = acc_a + exchange(send_a, 1, 1).astype(F32)
    acc_b = acc_b + exchange(send_b, 1, 1).astype(F32)
    orders_a, orders_b = hop_orders(lon_count)
    for step, (hops_a, hops_b) in enumerate(zip(orders_a, orders_b)):
        got_a = exchange(acc_a.astype(BF16), *hops_a)
        got_b = exchange(acc_b.astype(BF16), *hops_b)
        if step < len(orders_a) - 1:
            acc_a = acc_a + got_a.astype(F32)
            acc_b = acc_b + got_b.astype(F32)

    mine = pl.pallas_call(
        functools.partial(legendre_kernel, rows),
        out_shape=jax.ShapeDtypeStruct((2 * packed_rows, channels), BF16),
        in_specs=[whole] * 4,
        out_specs=whole,
        compiler_params=params,
    )(acc_a, got_a, acc_b, got_b)
    other = exchange(mine, 1, 1)

    block_rows = 2 * wave_dev * samples
    mixed, grad = pl.pallas_call(
        functools.partial(mixing_kernel, lon_count, wave_dev, samples),
        out_shape=(
            jax.ShapeDtypeStruct((degrees * block_rows * 2, LANES), BF16),
            jax.ShapeDtypeStruct((channels // lon_count, degrees, channels), F32),
        ),
        in_specs=[scalar] + [whole] * 3,
        out_specs=(whole, whole),
        scratch_shapes=[
            pltpu.VMEM((2, packed_rows * 2, LANES), F32),
            pltpu.VMEM((degrees * block_rows * 2, LANES), F32),
        ],
        compiler_params=params,
    )(where, mine, other, mixing)
    mixed = mixed.reshape(degrees, wave_dev, 2, 2, samples, LANES).transpose(0, 1, 2, 4, 3, 5)
    return mixed.reshape(degrees, wave_dev, 2, samples, channels), grad


def hop_orders(lon_count):
    bits = [1 << k for k in range(1, lon_count.bit_length() - 1)]
    bits[-1] += bits[-2]
    bits = [bit + 1 for bit in bits]
    half = len(bits) // 2
    near, far = bits[:half], bits[half:]
    chain_a = list(zip(near + far, far + near))
    chain_b = list(zip(near[::-1] + far[::-1], far[::-1] + near[::-1]))
    return chain_a, chain_b


def few_waves(mesh, fields, legendre):
    samples, rows, longitudes, channels = fields.shape
    waves, degrees = legendre.shape[1:]
    count = mesh.shape["lon"]
    return (
        mesh.shape["lat"] == 1
        and samples == 2
        and count >= 8
        and count & (count - 1) == 0
        and degrees == TILE
        and degrees <= waves
        and rows % TILE == 0
        and 2 * rows * (degrees // 2 + 1) <= channels
        and channels == 2 * LANES
        and channels // count == TILE
        and longitudes % 4 == 0
        and (4 * waves // count) % TILE == 0
    )


def solution(mesh):
    placed = (
        P(None, "lat", "lon", None),
        P("lat", "lon", None),
        P("lat", None, None),
        P("lat", "lon", None, None, None),
    )

    def program(fields, legendre, mixing, cotangent):
        body = sparse_shards if few_waves(mesh, fields, legendre) else dense_shards
        return jax.shard_map(
            body,
            mesh=mesh,
            in_specs=placed,
            out_specs=(P("lat", "lon", None, None, None), P("lon", "lat", None)),
            check_vma=False,
        )(fields, legendre, mixing, cotangent)

    return program
```

```python
import functools
import math

import jax
import jax.numpy as jnp
from jax import lax
from jax.experimental import pallas as pl
from jax.experimental.pallas import tpu as pltpu
from jax.sharding import PartitionSpec as P

F32 = jnp.float32
BF16 = jnp.bfloat16
TILE = 8
LANES = 128
VMEM_BYTES = 32 * 1024 * 1024


def dense_shards(fields, legendre, mixing, cotangent):
    samples = fields.shape[0]
    lat_rows = fields.shape[1]
    lon_cells = fields.shape[2]
    channels = fields.shape[3]
    lon_count = lax.axis_size("lon")
    lat_count = lax.axis_size("lat")
    nlon_total = lon_cells * lon_count
    wave_dev = legendre.shape[1]
    wave_total = wave_dev * lon_count
    degrees = legendre.shape[2]
    degree_dev = degrees // lat_count
    column_rows = 2 * wave_dev * samples
    column_width = 2 * samples * channels
    positions = jnp.arange(nlon_total, dtype=jnp.int32)
    wavenums = jnp.arange(wave_total, dtype=jnp.int32)
    phase = (positions[:, None] * wavenums[None, :] % nlon_total).astype(jnp.float32) * (
        2.0 * math.pi / nlon_total
    )
    fourier = jnp.stack([jnp.cos(phase), -jnp.sin(phase)], axis=2).reshape(
        nlon_total, 2 * wave_total
    )
    fourier = fourier * (1.0 / nlon_total**0.5)
    fourier_hi = fourier.astype(jnp.bfloat16)
    fourier_lo = (fourier - fourier_hi.astype(jnp.float32)).astype(jnp.bfloat16)
    portion = lax.all_to_all(fields, "lon", split_axis=3, concat_axis=2, tiled=True)
    spectrum = jnp.einsum("bjkc,kf->jfbc", portion, fourier_hi, preferred_element_type=jnp.float32)
    spectrum = spectrum + jnp.einsum(
        "bjkc,kf->jfbc", portion, fourier_lo, preferred_element_type=jnp.float32
    )
    owned = lax.all_to_all(spectrum, "lon", split_axis=1, concat_axis=3, tiled=True)
    spectral = owned.reshape(owned.shape[0], column_rows, channels)
    wave_global = lax.axis_index("lon") * wave_dev + jnp.arange(wave_dev, dtype=jnp.int32)
    degree_ids = jnp.arange(degrees, dtype=jnp.int32)
    keep = degree_ids[None, None, :] >= wave_global[None, :, None]
    basis = jnp.where(keep, legendre, jnp.float32(0.0))
    spectral_waves = spectral.reshape(lat_rows, wave_dev, column_width)
    summed = lax.psum_scatter(
        jnp.einsum("jml,jmq->lmq", basis, spectral_waves, precision=lax.Precision.HIGHEST),
        "lat",
        scatter_dimension=0,
        tiled=True,
    )
    coef = summed.reshape(degree_dev, column_rows, channels)
    coef_bf = coef.astype(jnp.bfloat16)
    mixed = jnp.einsum("lrc,lcd->lrd", coef_bf, mixing, preferred_element_type=jnp.float32)
    mixed = mixed.astype(jnp.bfloat16).reshape(degree_dev, wave_dev, 2, samples, channels)
    cot_rows = cotangent.reshape(degree_dev, column_rows, channels)
    weight_grad = lax.psum_scatter(
        jnp.einsum("lrc,lrd->cld", coef_bf, cot_rows, preferred_element_type=jnp.float32),
        "lon",
        scatter_dimension=0,
        tiled=True,
    )
    return (mixed, weight_grad)


def tile_slots(degrees):
    slots = []
    for group in range(degrees // 2 + 1):
        for place in range(degrees):
            if place >= group:
                slots.append((group, place))
            elif group < degrees - group:
                slots.append((degrees - group, place + degrees - group))
            else:
                slots.append(None)
    return slots


def packed_tiles(wave_dev, index, cots, legendre_ref, table_ref):
    degrees, rows = legendre_ref.shape[1:]
    slots = tile_slots(degrees)
    row = lax.broadcasted_iota(jnp.int32, (TILE, LANES), 0)
    zeros = jnp.zeros((TILE, LANES), F32)
    owned = [index == owner for owner in range((degrees - 1) // wave_dev + 1)]

    def cotangent(slot):
        if slot is None:
            return zeros
        wave, degree = slot
        at = (degree * wave_dev + wave % wave_dev) * TILE
        return jnp.where(owned[wave // wave_dev], cots[at : at + TILE], 0.0)

    upper = row < TILE // 2
    parts = ([], [])
    for pair in range(len(slots) // 2):
        one, two = cotangent(slots[2 * pair]), cotangent(slots[2 * pair + 1])
        parts[0].append(jnp.where(upper, one, pltpu.roll(two, TILE // 2, 0)))
        parts[1].append(jnp.where(upper, pltpu.roll(one, TILE // 2, 0), two))

    table_ref[...] = jnp.zeros(table_ref.shape, F32)
    table_ref[:, :, pl.ds(0, rows)] = legendre_ref[...]

    def basis(wave):
        block = jnp.where(owned[wave // wave_dev], table_ref[wave % wave_dev], 0.0)
        return jnp.where(row >= wave, block, 0.0)

    table = jnp.zeros((degrees, 2 * LANES), F32)
    for group in range(degrees // 2 + 1):
        block = basis(group)
        if 0 < group < degrees - group:
            rest = pltpu.roll(basis(degrees - group), group, 0)
            block = block + pltpu.roll(rest, rows, 1)
        block = jnp.concatenate([block, zeros], axis=1)
        table = table + (pltpu.roll(block, 2 * rows * group, 1) if group else block)
    high = table.astype(BF16).astype(F32)

    half = len(slots) // 4
    whole = []
    for tiles in parts:
        lanes = [tiles[lane * half : (lane + 1) * half] for lane in range(2)]
        cots = jnp.concatenate([jnp.concatenate(lane, axis=0) for lane in lanes], axis=1)
        whole.append(jnp.concatenate([cots, high, table - high], axis=0))
    return whole


def side_of(index, lon_count):
    side = index
    for bit in range(1, lon_count.bit_length() - 2):
        side = side ^ (index >> bit)
    return side & 1


def fourier_kernel(
    lon_count,
    where_ref,
    fields_ref,
    legendre_ref,
    cot_ref,
    first_ref,
    second_ref,
    first_send_ref,
    second_send_ref,
    grid_ref,
    values_ref,
    cots_ref,
    total_ref,
    table_ref,
    sems,
):
    rows, cells, channels = fields_ref.shape[1:]
    wave_dev, degrees = legendre_ref.shape[:2]
    parts = 2 * degrees
    spec_rows = parts * rows
    nlon_total = cells * lon_count
    index = where_ref[0]
    side = side_of(index, lon_count)
    copies = [
        pltpu.make_async_copy(fields_ref.at[sample], grid_ref.at[k], sems.at[k])
        for k, sample in enumerate((1 - side, side))
    ]
    for copy in copies:
        copy.start()
    owns = index < (degrees - 1) // wave_dev + 1
    others = [
        pltpu.make_async_copy(legendre_ref, values_ref, sems.at[2]),
        pltpu.make_async_copy(cot_ref, cots_ref, sems.at[3]),
    ]

    @pl.when(owns)
    def _():
        for copy in others:
            copy.start()

    width = TILE * cells
    column = lax.broadcasted_iota(jnp.int32, (parts, width), 1)
    part = lax.broadcasted_iota(jnp.int32, (parts, width), 0)
    cell = index * cells + lax.rem(column, cells)
    turn = lax.rem(cell * (part // 2) + lax.rem(part, 2) * (nlon_total // 4), nlon_total)
    wave = jnp.cos(turn.astype(F32) * (2.0 * math.pi / nlon_total)) * (1.0 / nlon_total**0.5)
    spread = (parts, TILE, width)
    own_row = (
        lax.broadcasted_iota(jnp.int32, spread, 2) // cells
        == lax.broadcasted_iota(jnp.int32, spread, 1)
    )
    wave = jnp.where(own_row, jnp.broadcast_to(wave[:, None, :], spread), 0.0)
    wave = wave.reshape(parts * TILE, width)
    wave_hi = wave.astype(BF16)
    wave_lo = (wave - wave_hi.astype(F32)).astype(BF16)
    cut = first_ref.shape[0] // rows
    kept = (parts - cut) * rows
    rest = pl.ds(kept, second_ref.shape[0] - kept)

    @pl.when(owns)
    def _():
        for copy in others:
            copy.wait()
        cots = cots_ref[...].astype(F32)
        real, imag = packed_tiles(wave_dev, index, cots, values_ref, table_ref)
        second_ref[rest, :] = jnp.where(side == 0, real, imag)
        second_send_ref[rest, :] = jnp.where(side == 0, imag, real).astype(BF16)

    @pl.when(jnp.logical_not(owns))
    def _():
        second_ref[rest, :] = jnp.zeros((rest.size, channels), F32)
        second_send_ref[rest, :] = jnp.zeros((rest.size, channels), BF16)


    for copy in copies:
        copy.wait()
    for k, first in [(k, first) for k in range(2) for first in range(0, rows, TILE)]:
        grid = grid_ref[k, pl.ds(first, TILE)].astype(F32).reshape(width, channels).astype(BF16)
        sums = jnp.dot(wave_hi, grid, preferred_element_type=F32)
        sums = sums + jnp.dot(wave_lo, grid, preferred_element_type=F32)
        for part in range(parts):
            tile = sums[part * TILE : (part + 1) * TILE]
            if k == 0:
                total_ref[pl.ds(part * rows + first, TILE), :] = tile
            elif part < cut:
                first_ref[pl.ds(part * rows + first, TILE), :] = tile
            else:
                second_ref[pl.ds((part - cut) * rows + first, TILE), :] = tile
        if k == 0 and first + TILE == rows:
            first_send_ref[...] = total_ref[pl.ds(0, cut * rows), :].astype(BF16)
            second_send_ref[pl.ds(0, kept), :] = total_ref[pl.ds(cut * rows, kept), :].astype(BF16)


def legendre_kernel(
    rows, first_ref, first_got_ref, second_ref, second_got_ref, out_ref
):
    degrees = TILE
    groups = degrees // 2 + 1
    first = first_ref[...] + first_got_ref[...].astype(F32)
    second = second_ref[...] + second_got_ref[...].astype(F32)
    spec_rows = 2 * degrees * rows
    spec = jnp.concatenate([first, second], axis=0)
    packed = groups * 2 * degrees
    table = spec[spec_rows + packed :]
    spec_hi = spec[:spec_rows].astype(BF16).astype(F32)
    spec_lo = spec[:spec_rows] - spec_hi
    coefs = []
    for part in range(2):
        for group in range(groups):
            basis = table[:, 2 * rows * group : 2 * rows * (group + 1)].astype(BF16)
            partner = degrees - group if 0 < group < degrees - group else group
            low = (2 * group + part) * rows
            high = (2 * partner + part) * rows
            block, rest = (
                jnp.concatenate([half[low : low + rows], half[high : high + rows]], axis=0)
                for half in (spec_hi, spec_lo)
            )
            sums = jnp.dot(basis, block.astype(BF16), preferred_element_type=F32)
            more = jnp.dot(basis[:degrees], rest.astype(BF16), preferred_element_type=F32)
            coefs.append(sums[:degrees] + sums[degrees:] + more)
    coefs.append(spec[spec_rows : spec_rows + packed])
    out_ref[...] = jnp.concatenate(coefs, axis=0).astype(BF16)


def mixing_kernel(
    lon_count, wave_dev, samples, where_ref, mine_ref, other_ref, mixing_ref, mixed_ref, grad_ref, cot_ref, out_ref
):
    degrees, channels = mixing_ref.shape[:2]
    groups = degrees // 2 + 1
    slots = groups * degrees
    terms = 2 * samples * slots
    index = where_ref[0]
    side = side_of(index, lon_count)
    mine, other = mine_ref[...].astype(F32), other_ref[...].astype(F32)
    held = [jnp.where(side == k, mine, other) for k in range(2)]
    coef = [held[sample][part * slots : (part + 1) * slots] for part in range(2) for sample in range(2)]
    coef = jnp.concatenate(coef, axis=0).astype(BF16)
    cots = []
    for part in range(2):
        packed = held[part][2 * slots :]
        for lane in range(2):
            half = packed[:, lane * LANES : (lane + 1) * LANES]
            cot_ref[part, pl.ds(lane * packed.shape[0], packed.shape[0]), :] = half
        for sample in range(samples):
            halves = [
                cot_ref[part, pl.ds(2 * lane + sample, slots, stride=2 * samples), :]
                for lane in range(2)
            ]
            cots.append(jnp.concatenate(halves, axis=1))
    cot = jnp.concatenate(cots, axis=0).astype(BF16)

    block = 2 * TILE
    shape = (block, terms)
    row = lax.broadcasted_iota(jnp.int32, shape, 0)
    term = lax.broadcasted_iota(jnp.int32, shape, 1)
    wave = index * wave_dev + row // 2
    tile = jnp.where(wave < groups, wave * degrees, (degrees - wave) * degrees - wave)
    base = row % 2 * (samples * slots) + tile
    chosen = []
    for degree in range(degrees):
        for sample in range(samples):
            hit = jnp.where(wave <= degree, base + (sample * slots + degree), -1)
            chosen.append(jnp.where(term == hit, 1.0, 0.0).astype(BF16))
    chosen = jnp.concatenate(chosen, axis=0)
    lhs = jnp.dot(chosen, coef, preferred_element_type=F32).astype(BF16)
    count = 2 * wave_dev
    for degree in range(degrees):
        at = degree * samples * block
        mixed = jnp.dot(
            lhs[at : at + samples * block], mixing_ref[degree], preferred_element_type=F32
        )
        for sample in range(samples):
            for lane in range(2):
                part = mixed[sample * block : sample * block + count, lane * LANES : (lane + 1) * LANES]
                at = degree * 2 * samples * count + 2 * lane + sample
                out_ref[pl.ds(at, count, stride=2 * samples), :] = part
    mixed_ref[...] = out_ref[...].astype(BF16)

    own = grad_ref.shape[0]
    channel = lax.broadcasted_iota(jnp.int32, (own, channels), 1)
    row = lax.broadcasted_iota(jnp.int32, (own, channels), 0)
    pick = jnp.where(channel == index * own + row, 1.0, 0.0).astype(BF16)
    turned = lax.dot_general(
        pick, coef, (((1,), (1,)), ((), ())), preferred_element_type=F32
    )
    shape = (degrees, terms)
    slot = lax.broadcasted_iota(jnp.int32, shape, 1) % slots
    place, group = slot % degrees, slot // degrees
    degree = jnp.where(place >= group, place, place + degrees - group)
    of_degree = degree == lax.broadcasted_iota(jnp.int32, shape, 0)
    turned = [jnp.where(of_degree, turned[k : k + 1], 0.0) for k in range(own)]
    turned = jnp.concatenate(turned, axis=0).astype(BF16)
    grad = jnp.dot(turned, cot, preferred_element_type=F32)
    grad_ref[...] = grad.reshape(own, degrees, channels)


def sparse_shards(fields, legendre, mixing, cotangent):
    samples, rows, cells, channels = fields.shape
    lon_count = lax.axis_size("lon")
    wave_dev, degrees = legendre.shape[1:]
    parts = 2 * degrees
    spec_rows = parts * rows
    packed_rows = (degrees // 2 + 1) * parts
    index = lax.axis_index("lon")
    where = index.reshape(1).astype(jnp.int32)
    whole = pl.BlockSpec(memory_space=pltpu.VMEM)
    scalar = pl.BlockSpec(memory_space=pltpu.SMEM)
    params = pltpu.CompilerParams(vmem_limit_bytes=VMEM_BYTES)

    def in_hbm(array):
        return pltpu.with_memory_space_constraint(array, pltpu.HBM)

    def exchange(array, *hops):
        pairs = [(i, i ^ hops[side_of(i, lon_count)]) for i in range(lon_count)]
        return lax.ppermute(array, "lon", pairs)

    cut = (parts // 2 + 3) * rows
    rest = spec_rows - cut + packed_rows + 2 * TILE
    halves = cotangent.reshape(degrees, wave_dev, 2, samples, 2, LANES)
    halves = halves.transpose(0, 1, 2, 4, 3, 5).reshape(-1, LANES)
    far = pl.BlockSpec(memory_space=pltpu.HBM)
    acc_a, acc_b, send_a, send_b = pl.pallas_call(
        functools.partial(fourier_kernel, lon_count),
        out_shape=(
            jax.ShapeDtypeStruct((cut, channels), F32),
            jax.ShapeDtypeStruct((rest, channels), F32),
            jax.ShapeDtypeStruct((cut, channels), BF16),
            jax.ShapeDtypeStruct((rest, channels), BF16),
        ),
        in_specs=[scalar, far, far, far],
        out_specs=(whole, whole, whole, whole),
        scratch_shapes=[
            pltpu.VMEM(fields.shape, BF16),
            pltpu.VMEM((wave_dev, degrees, rows), F32),
            pltpu.VMEM(halves.shape, BF16),
            pltpu.VMEM((spec_rows, channels), F32),
            pltpu.VMEM((wave_dev, degrees, LANES), F32),
            pltpu.SemaphoreType.DMA((4,)),
        ],
        compiler_params=params,
    )(where, in_hbm(fields), in_hbm(legendre.transpose(1, 2, 0)), in_hbm(halves))

    acc_a = acc_a + exchange(send_a, 1, 1).astype(F32)
    acc_b = acc_b + exchange(send_b, 1, 1).astype(F32)
    orders_a, orders_b = hop_orders(lon_count)
    for step, (hops_a, hops_b) in enumerate(zip(orders_a, orders_b)):
        got_a = exchange(acc_a.astype(BF16), *hops_a)
        got_b = exchange(acc_b.astype(BF16), *hops_b)
        if step < len(orders_a) - 1:
            acc_a = acc_a + got_a.astype(F32)
            acc_b = acc_b + got_b.astype(F32)

    mine = pl.pallas_call(
        functools.partial(legendre_kernel, rows),
        out_shape=jax.ShapeDtypeStruct((2 * packed_rows, channels), BF16),
        in_specs=[whole] * 4,
        out_specs=whole,
        compiler_params=params,
    )(acc_a, got_a, acc_b, got_b)
    other = exchange(mine, 1, 1)

    block_rows = 2 * wave_dev * samples
    mixed, grad = pl.pallas_call(
        functools.partial(mixing_kernel, lon_count, wave_dev, samples),
        out_shape=(
            jax.ShapeDtypeStruct((degrees * block_rows * 2, LANES), BF16),
            jax.ShapeDtypeStruct((channels // lon_count, degrees, channels), F32),
        ),
        in_specs=[scalar] + [whole] * 3,
        out_specs=(whole, whole),
        scratch_shapes=[
            pltpu.VMEM((2, packed_rows * 2, LANES), F32),
            pltpu.VMEM((degrees * block_rows * 2, LANES), F32),
        ],
        compiler_params=params,
    )(where, mine, other, mixing)
    mixed = mixed.reshape(degrees, wave_dev, 2, 2, samples, LANES).transpose(0, 1, 2, 4, 3, 5)
    return mixed.reshape(degrees, wave_dev, 2, samples, channels), grad


def hop_orders(lon_count):
    bits = [1 << k for k in range(1, lon_count.bit_length() - 1)]
    bits[-1] += bits[-2]
    bits = [bit + 1 for bit in bits]
    half = len(bits) // 2
    near, far = bits[:half], bits[half:]
    one = [hop for pair in zip(near, far) for hop in pair]
    two = [hop for pair in zip(far, near) for hop in pair]
    chain_a = list(zip(one, two))
    chain_b = list(zip(one[half:] + one[:half][::-1], two[half:] + two[:half][::-1]))
    return chain_a, chain_b


def few_waves(mesh, fields, legendre):
    samples, rows, longitudes, channels = fields.shape
    waves, degrees = legendre.shape[1:]
    count = mesh.shape["lon"]
    return (
        mesh.shape["lat"] == 1
        and samples == 2
        and count >= 8
        and count & (count - 1) == 0
        and count.bit_length() % 2 == 0
        and degrees == TILE
        and degrees <= waves
        and rows % TILE == 0
        and 2 * rows * (degrees // 2 + 1) <= channels
        and channels == 2 * LANES
        and channels // count == TILE
        and longitudes % 4 == 0
        and (4 * waves // count) % TILE == 0
    )


def solution(mesh):
    placed = (
        P(None, "lat", "lon", None),
        P("lat", "lon", None),
        P("lat", None, None),
        P("lat", "lon", None, None, None),
    )

    def program(fields, legendre, mixing, cotangent):
        body = sparse_shards if few_waves(mesh, fields, legendre) else dense_shards
        return jax.shard_map(
            body,
            mesh=mesh,
            in_specs=placed,
            out_specs=(P("lat", "lon", None, None, None), P("lon", "lat", None)),
            check_vma=False,
        )(fields, legendre, mixing, cotangent)

    return program
```

```python
import functools
import math

import jax
import jax.numpy as jnp
from jax import lax
from jax.experimental import pallas as pl
from jax.experimental.pallas import tpu as pltpu
from jax.sharding import PartitionSpec as P

F32 = jnp.float32
BF16 = jnp.bfloat16
TILE = 8
LANES = 128
VMEM_BYTES = 32 * 1024 * 1024


def dense_shards(fields, legendre, mixing, cotangent):
    samples = fields.shape[0]
    lat_rows = fields.shape[1]
    lon_cells = fields.shape[2]
    channels = fields.shape[3]
    lon_count = lax.axis_size("lon")
    lat_count = lax.axis_size("lat")
    nlon_total = lon_cells * lon_count
    wave_dev = legendre.shape[1]
    wave_total = wave_dev * lon_count
    degrees = legendre.shape[2]
    degree_dev = degrees // lat_count
    column_rows = 2 * wave_dev * samples
    column_width = 2 * samples * channels
    positions = jnp.arange(nlon_total, dtype=jnp.int32)
    wavenums = jnp.arange(wave_total, dtype=jnp.int32)
    phase = (positions[:, None] * wavenums[None, :] % nlon_total).astype(jnp.float32) * (
        2.0 * math.pi / nlon_total
    )
    fourier = jnp.stack([jnp.cos(phase), -jnp.sin(phase)], axis=2).reshape(
        nlon_total, 2 * wave_total
    )
    fourier = fourier * (1.0 / nlon_total**0.5)
    fourier_hi = fourier.astype(jnp.bfloat16)
    fourier_lo = (fourier - fourier_hi.astype(jnp.float32)).astype(jnp.bfloat16)
    portion = lax.all_to_all(fields, "lon", split_axis=3, concat_axis=2, tiled=True)
    spectrum = jnp.einsum("bjkc,kf->jfbc", portion, fourier_hi, preferred_element_type=jnp.float32)
    spectrum = spectrum + jnp.einsum(
        "bjkc,kf->jfbc", portion, fourier_lo, preferred_element_type=jnp.float32
    )
    owned = lax.all_to_all(spectrum, "lon", split_axis=1, concat_axis=3, tiled=True)
    spectral = owned.reshape(owned.shape[0], column_rows, channels)
    wave_global = lax.axis_index("lon") * wave_dev + jnp.arange(wave_dev, dtype=jnp.int32)
    degree_ids = jnp.arange(degrees, dtype=jnp.int32)
    keep = degree_ids[None, None, :] >= wave_global[None, :, None]
    basis = jnp.where(keep, legendre, jnp.float32(0.0))
    spectral_waves = spectral.reshape(lat_rows, wave_dev, column_width)
    summed = lax.psum_scatter(
        jnp.einsum("jml,jmq->lmq", basis, spectral_waves, precision=lax.Precision.HIGHEST),
        "lat",
        scatter_dimension=0,
        tiled=True,
    )
    coef = summed.reshape(degree_dev, column_rows, channels)
    coef_bf = coef.astype(jnp.bfloat16)
    mixed = jnp.einsum("lrc,lcd->lrd", coef_bf, mixing, preferred_element_type=jnp.float32)
    mixed = mixed.astype(jnp.bfloat16).reshape(degree_dev, wave_dev, 2, samples, channels)
    cot_rows = cotangent.reshape(degree_dev, column_rows, channels)
    weight_grad = lax.psum_scatter(
        jnp.einsum("lrc,lrd->cld", coef_bf, cot_rows, preferred_element_type=jnp.float32),
        "lon",
        scatter_dimension=0,
        tiled=True,
    )
    return (mixed, weight_grad)


def tile_slots(degrees):
    slots = []
    for group in range(degrees // 2 + 1):
        for place in range(degrees):
            if place >= group:
                slots.append((group, place))
            elif group < degrees - group:
                slots.append((degrees - group, place + degrees - group))
            else:
                slots.append(None)
    return slots


def packed_tiles(wave_dev, index, cots, legendre_ref, table_ref):
    degrees, rows = legendre_ref.shape[1:]
    slots = tile_slots(degrees)
    row = lax.broadcasted_iota(jnp.int32, (TILE, LANES), 0)
    zeros = jnp.zeros((TILE, LANES), F32)
    owned = [index == owner for owner in range((degrees - 1) // wave_dev + 1)]

    def cotangent(slot):
        if slot is None:
            return zeros
        wave, degree = slot
        at = (degree * wave_dev + wave % wave_dev) * TILE
        return jnp.where(owned[wave // wave_dev], cots[at : at + TILE], 0.0)

    upper = row < TILE // 2
    parts = ([], [])
    for pair in range(len(slots) // 2):
        one, two = cotangent(slots[2 * pair]), cotangent(slots[2 * pair + 1])
        parts[0].append(jnp.where(upper, one, pltpu.roll(two, TILE // 2, 0)))
        parts[1].append(jnp.where(upper, pltpu.roll(one, TILE // 2, 0), two))

    table_ref[...] = jnp.zeros(table_ref.shape, F32)
    table_ref[:, :, pl.ds(0, rows)] = legendre_ref[...]

    def basis(wave):
        block = jnp.where(owned[wave // wave_dev], table_ref[wave % wave_dev], 0.0)
        return jnp.where(row >= wave, block, 0.0)

    table = jnp.zeros((degrees, 2 * LANES), F32)
    for group in range(degrees // 2 + 1):
        block = basis(group)
        if 0 < group < degrees - group:
            rest = pltpu.roll(basis(degrees - group), group, 0)
            block = block + pltpu.roll(rest, rows, 1)
        block = jnp.concatenate([block, zeros], axis=1)
        table = table + (pltpu.roll(block, 2 * rows * group, 1) if group else block)
    high = table.astype(BF16).astype(F32)

    half = len(slots) // 4
    whole = []
    for tiles in parts:
        lanes = [tiles[lane * half : (lane + 1) * half] for lane in range(2)]
        cots = jnp.concatenate([jnp.concatenate(lane, axis=0) for lane in lanes], axis=1)
        whole.append(jnp.concatenate([cots, high, table - high], axis=0))
    return whole


def side_of(index, lon_count):
    side = index
    for bit in range(1, lon_count.bit_length() - 2):
        side = side ^ (index >> bit)
    return side & 1


def fourier_kernel(
    lon_count,
    where_ref,
    fields_ref,
    legendre_ref,
    cot_ref,
    first_ref,
    second_ref,
    first_send_ref,
    second_send_ref,
    grid_ref,
    values_ref,
    cots_ref,
    total_ref,
    table_ref,
    sems,
):
    channels = fields_ref.shape[2]
    wave_dev, degrees, rows = legendre_ref.shape
    cells = fields_ref.shape[1] // rows
    parts = 2 * degrees
    spec_rows = parts * rows
    nlon_total = cells * lon_count
    index = where_ref[0]
    side = side_of(index, lon_count)
    copies = [
        pltpu.make_async_copy(fields_ref.at[sample], grid_ref.at[k], sems.at[k])
        for k, sample in enumerate((1 - side, side))
    ]
    for copy in copies:
        copy.start()
    owns = index < (degrees - 1) // wave_dev + 1
    others = [
        pltpu.make_async_copy(legendre_ref, values_ref, sems.at[2]),
        pltpu.make_async_copy(cot_ref, cots_ref, sems.at[3]),
    ]

    @pl.when(owns)
    def _():
        for copy in others:
            copy.start()

    width = TILE * cells
    column = lax.broadcasted_iota(jnp.int32, (parts, width), 1)
    part = lax.broadcasted_iota(jnp.int32, (parts, width), 0)
    cell = index * cells + lax.rem(column, cells)
    turn = lax.rem(cell * (part // 2) + lax.rem(part, 2) * (nlon_total // 4), nlon_total)
    wave = jnp.cos(turn.astype(F32) * (2.0 * math.pi / nlon_total)) * (1.0 / nlon_total**0.5)
    spread = (parts, TILE, width)
    own_row = (
        lax.broadcasted_iota(jnp.int32, spread, 2) // cells
        == lax.broadcasted_iota(jnp.int32, spread, 1)
    )
    wave = jnp.where(own_row, jnp.broadcast_to(wave[:, None, :], spread), 0.0)
    wave = wave.reshape(parts * TILE, width)
    wave_hi = wave.astype(BF16)
    wave_lo = (wave - wave_hi.astype(F32)).astype(BF16)
    cut = first_ref.shape[0] // rows
    kept = (parts - cut) * rows
    rest = pl.ds(kept, second_ref.shape[0] - kept)

    @pl.when(owns)
    def _():
        for copy in others:
            copy.wait()
        cots = cots_ref[...].astype(F32)
        real, imag = packed_tiles(wave_dev, index, cots, values_ref, table_ref)
        second_ref[rest, :] = jnp.where(side == 0, real, imag)
        total_ref[pl.ds(spec_rows, rest.size), :] = jnp.where(side == 0, imag, real)

    @pl.when(jnp.logical_not(owns))
    def _():
        second_ref[rest, :] = jnp.zeros((rest.size, channels), F32)
        total_ref[pl.ds(spec_rows, rest.size), :] = jnp.zeros((rest.size, channels), F32)

    for copy in copies:
        copy.wait()
    for k, first in [(k, first) for k in range(2) for first in range(0, rows, TILE)]:
        grid = grid_ref[k, pl.ds(first * cells, width), :]
        sums = jnp.dot(wave_hi, grid, preferred_element_type=F32)
        sums = sums + jnp.dot(wave_lo, grid, preferred_element_type=F32)
        for part in range(parts):
            tile = sums[part * TILE : (part + 1) * TILE]
            if k == 0:
                total_ref[pl.ds(part * rows + first, TILE), :] = tile
            elif part < cut:
                first_ref[pl.ds(part * rows + first, TILE), :] = tile
            else:
                second_ref[pl.ds((part - cut) * rows + first, TILE), :] = tile
        if k == 0 and first + TILE == rows:
            first_send_ref[...] = total_ref[pl.ds(0, cut * rows), :].astype(BF16)
            after = pl.ds(cut * rows, second_send_ref.shape[0])
            second_send_ref[...] = total_ref[after, :].astype(BF16)


def legendre_kernel(
    rows, first_ref, first_got_ref, second_ref, second_got_ref, out_ref
):
    degrees = TILE
    groups = degrees // 2 + 1
    first = first_ref[...] + first_got_ref[...].astype(F32)
    second = second_ref[...] + second_got_ref[...].astype(F32)
    spec_rows = 2 * degrees * rows
    spec = jnp.concatenate([first, second], axis=0)
    packed = groups * 2 * degrees
    table = spec[spec_rows + packed :]
    spec_hi = spec[:spec_rows].astype(BF16).astype(F32)
    spec_lo = spec[:spec_rows] - spec_hi
    coefs = []
    for part in range(2):
        for group in range(groups):
            basis = table[:, 2 * rows * group : 2 * rows * (group + 1)].astype(BF16)
            partner = degrees - group if 0 < group < degrees - group else group
            low = (2 * group + part) * rows
            high = (2 * partner + part) * rows
            block, rest = (
                jnp.concatenate([half[low : low + rows], half[high : high + rows]], axis=0)
                for half in (spec_hi, spec_lo)
            )
            sums = jnp.dot(basis, block.astype(BF16), preferred_element_type=F32)
            more = jnp.dot(basis[:degrees], rest.astype(BF16), preferred_element_type=F32)
            coefs.append(sums[:degrees] + sums[degrees:] + more)
    coefs.append(spec[spec_rows : spec_rows + packed])
    out_ref[...] = jnp.concatenate(coefs, axis=0).astype(BF16)


def mixing_kernel(
    lon_count, wave_dev, samples, where_ref, mine_ref, other_ref, mixing_ref, mixed_ref, grad_ref, cot_ref, out_ref
):
    degrees, channels = mixing_ref.shape[:2]
    groups = degrees // 2 + 1
    slots = groups * degrees
    terms = 2 * samples * slots
    index = where_ref[0]
    side = side_of(index, lon_count)
    mine, other = mine_ref[...].astype(F32), other_ref[...].astype(F32)
    held = [jnp.where(side == k, mine, other) for k in range(2)]
    coef = [held[sample][part * slots : (part + 1) * slots] for part in range(2) for sample in range(2)]
    coef = jnp.concatenate(coef, axis=0).astype(BF16)
    cots = []
    for part in range(2):
        packed = held[part][2 * slots :]
        for lane in range(2):
            half = packed[:, lane * LANES : (lane + 1) * LANES]
            cot_ref[part, pl.ds(lane * packed.shape[0], packed.shape[0]), :] = half
        for sample in range(samples):
            halves = [
                cot_ref[part, pl.ds(2 * lane + sample, slots, stride=2 * samples), :]
                for lane in range(2)
            ]
            cots.append(jnp.concatenate(halves, axis=1))
    cot = jnp.concatenate(cots, axis=0).astype(BF16)

    block = 2 * TILE
    shape = (block, terms)
    row = lax.broadcasted_iota(jnp.int32, shape, 0)
    term = lax.broadcasted_iota(jnp.int32, shape, 1)
    wave = index * wave_dev + row // 2
    tile = jnp.where(wave < groups, wave * degrees, (degrees - wave) * degrees - wave)
    base = row % 2 * (samples * slots) + tile
    chosen = []
    for degree in range(degrees):
        for sample in range(samples):
            hit = jnp.where(wave <= degree, base + (sample * slots + degree), -1)
            chosen.append(jnp.where(term == hit, 1.0, 0.0).astype(BF16))
    chosen = jnp.concatenate(chosen, axis=0)
    lhs = jnp.dot(chosen, coef, preferred_element_type=F32).astype(BF16)
    count = 2 * wave_dev
    for degree in range(degrees):
        at = degree * samples * block
        mixed = jnp.dot(
            lhs[at : at + samples * block], mixing_ref[degree], preferred_element_type=F32
        )
        for sample in range(samples):
            for lane in range(2):
                part = mixed[sample * block : sample * block + count, lane * LANES : (lane + 1) * LANES]
                at = degree * 2 * samples * count + 2 * lane + sample
                out_ref[pl.ds(at, count, stride=2 * samples), :] = part
    mixed_ref[...] = out_ref[...].astype(BF16)

    own = grad_ref.shape[0]
    channel = lax.broadcasted_iota(jnp.int32, (own, channels), 1)
    row = lax.broadcasted_iota(jnp.int32, (own, channels), 0)
    pick = jnp.where(channel == index * own + row, 1.0, 0.0).astype(BF16)
    turned = lax.dot_general(
        pick, coef, (((1,), (1,)), ((), ())), preferred_element_type=F32
    )
    shape = (degrees, terms)
    slot = lax.broadcasted_iota(jnp.int32, shape, 1) % slots
    place, group = slot % degrees, slot // degrees
    degree = jnp.where(place >= group, place, place + degrees - group)
    of_degree = degree == lax.broadcasted_iota(jnp.int32, shape, 0)
    turned = [jnp.where(of_degree, turned[k : k + 1], 0.0) for k in range(own)]
    turned = jnp.concatenate(turned, axis=0).astype(BF16)
    grad = jnp.dot(turned, cot, preferred_element_type=F32)
    grad_ref[...] = grad.reshape(own, degrees, channels)


def sparse_shards(fields, legendre, mixing, cotangent):
    samples, rows, cells, channels = fields.shape
    lon_count = lax.axis_size("lon")
    wave_dev, degrees = legendre.shape[1:]
    parts = 2 * degrees
    spec_rows = parts * rows
    packed_rows = (degrees // 2 + 1) * parts
    index = lax.axis_index("lon")
    where = index.reshape(1).astype(jnp.int32)
    whole = pl.BlockSpec(memory_space=pltpu.VMEM)
    scalar = pl.BlockSpec(memory_space=pltpu.SMEM)
    params = pltpu.CompilerParams(vmem_limit_bytes=VMEM_BYTES)

    def in_hbm(array):
        return pltpu.with_memory_space_constraint(array, pltpu.HBM)

    def exchange(array, *hops):
        pairs = [(i, i ^ hops[side_of(i, lon_count)]) for i in range(lon_count)]
        return lax.ppermute(array, "lon", pairs)

    cut = (parts // 2 + 3) * rows
    rest = spec_rows - cut + packed_rows + 2 * TILE
    halves = cotangent.reshape(degrees, wave_dev, 2, samples, 2, LANES)
    halves = halves.transpose(0, 1, 2, 4, 3, 5).reshape(-1, LANES)
    grid = fields.reshape(samples, rows * cells, channels)
    far = pl.BlockSpec(memory_space=pltpu.HBM)
    acc_a, acc_b, send_a, send_b = pl.pallas_call(
        functools.partial(fourier_kernel, lon_count),
        out_shape=(
            jax.ShapeDtypeStruct((cut, channels), F32),
            jax.ShapeDtypeStruct((rest, channels), F32),
            jax.ShapeDtypeStruct((cut, channels), BF16),
            jax.ShapeDtypeStruct((rest, channels), BF16),
        ),
        in_specs=[scalar, far, far, far],
        out_specs=(whole, whole, whole, whole),
        scratch_shapes=[
            pltpu.VMEM((samples, rows * cells, channels), BF16),
            pltpu.VMEM((wave_dev, degrees, rows), F32),
            pltpu.VMEM(halves.shape, BF16),
            pltpu.VMEM((cut + rest, channels), F32),
            pltpu.VMEM((wave_dev, degrees, LANES), F32),
            pltpu.SemaphoreType.DMA((4,)),
        ],
        compiler_params=params,
    )(where, in_hbm(grid), in_hbm(legendre.transpose(1, 2, 0)), in_hbm(halves))

    acc_a = acc_a + exchange(send_a, 1, 1).astype(F32)
    acc_b = acc_b + exchange(send_b, 1, 1).astype(F32)
    orders_a, orders_b = hop_orders(lon_count)
    for step, (hops_a, hops_b) in enumerate(zip(orders_a, orders_b)):
        got_a = exchange(acc_a.astype(BF16), *hops_a)
        got_b = exchange(acc_b.astype(BF16), *hops_b)
        if step < len(orders_a) - 1:
            acc_a = acc_a + got_a.astype(F32)
            acc_b = acc_b + got_b.astype(F32)

    mine = pl.pallas_call(
        functools.partial(legendre_kernel, rows),
        out_shape=jax.ShapeDtypeStruct((2 * packed_rows, channels), BF16),
        in_specs=[whole] * 4,
        out_specs=whole,
        compiler_params=params,
    )(acc_a, got_a, acc_b, got_b)
    other = exchange(mine, 1, 1)

    block_rows = 2 * wave_dev * samples
    mixed, grad = pl.pallas_call(
        functools.partial(mixing_kernel, lon_count, wave_dev, samples),
        out_shape=(
            jax.ShapeDtypeStruct((degrees * block_rows * 2, LANES), BF16),
            jax.ShapeDtypeStruct((channels // lon_count, degrees, channels), F32),
        ),
        in_specs=[scalar] + [whole] * 3,
        out_specs=(whole, whole),
        scratch_shapes=[
            pltpu.VMEM((2, packed_rows * 2, LANES), F32),
            pltpu.VMEM((degrees * block_rows * 2, LANES), F32),
        ],
        compiler_params=params,
    )(where, mine, other, mixing)
    mixed = mixed.reshape(degrees, wave_dev, 2, 2, samples, LANES).transpose(0, 1, 2, 4, 3, 5)
    return mixed.reshape(degrees, wave_dev, 2, samples, channels), grad


def hop_orders(lon_count):
    bits = [1 << k for k in range(1, lon_count.bit_length() - 1)]
    bits[-1] += bits[-2]
    bits = [bit + 1 for bit in bits]
    half = len(bits) // 2
    near, far = bits[:half], bits[half:]
    one = [hop for pair in zip(near, far) for hop in pair]
    two = [hop for pair in zip(far, near) for hop in pair]
    chain_a = list(zip(one, two))
    chain_b = list(zip(one[half:] + one[:half][::-1], two[half:] + two[:half][::-1]))
    return chain_a, chain_b


def few_waves(mesh, fields, legendre):
    samples, rows, longitudes, channels = fields.shape
    waves, degrees = legendre.shape[1:]
    count = mesh.shape["lon"]
    return (
        mesh.shape["lat"] == 1
        and samples == 2
        and count >= 8
        and count & (count - 1) == 0
        and count.bit_length() % 2 == 0
        and degrees == TILE
        and degrees <= waves
        and rows % TILE == 0
        and longitudes // count % 2 == 0
        and 2 * rows * (degrees // 2 + 1) <= channels
        and channels == 2 * LANES
        and channels // count == TILE
        and longitudes % 4 == 0
        and (4 * waves // count) % TILE == 0
    )


def solution(mesh):
    placed = (
        P(None, "lat", "lon", None),
        P("lat", "lon", None),
        P("lat", None, None),
        P("lat", "lon", None, None, None),
    )

    def program(fields, legendre, mixing, cotangent):
        body = sparse_shards if few_waves(mesh, fields, legendre) else dense_shards
        return jax.shard_map(
            body,
            mesh=mesh,
            in_specs=placed,
            out_specs=(P("lat", "lon", None, None, None), P("lon", "lat", None)),
            check_vma=False,
        )(fields, legendre, mixing, cotangent)

    return program
```

```python
import functools
import math

import jax
import jax.numpy as jnp
from jax import lax
from jax.experimental import pallas as pl
from jax.experimental.pallas import tpu as pltpu
from jax.sharding import PartitionSpec as P

F32 = jnp.float32
BF16 = jnp.bfloat16
TILE = 8
LANES = 128
VMEM_BYTES = 32 * 1024 * 1024
CHAINS = 3


def dense_shards(fields, legendre, mixing, cotangent):
    samples = fields.shape[0]
    lat_rows = fields.shape[1]
    lon_cells = fields.shape[2]
    channels = fields.shape[3]
    lon_count = lax.axis_size("lon")
    lat_count = lax.axis_size("lat")
    nlon_total = lon_cells * lon_count
    wave_dev = legendre.shape[1]
    wave_total = wave_dev * lon_count
    degrees = legendre.shape[2]
    degree_dev = degrees // lat_count
    column_rows = 2 * wave_dev * samples
    column_width = 2 * samples * channels
    positions = jnp.arange(nlon_total, dtype=jnp.int32)
    wavenums = jnp.arange(wave_total, dtype=jnp.int32)
    phase = (positions[:, None] * wavenums[None, :] % nlon_total).astype(jnp.float32) * (
        2.0 * math.pi / nlon_total
    )
    fourier = jnp.stack([jnp.cos(phase), -jnp.sin(phase)], axis=2).reshape(
        nlon_total, 2 * wave_total
    )
    fourier = fourier * (1.0 / nlon_total**0.5)
    fourier_hi = fourier.astype(jnp.bfloat16)
    fourier_lo = (fourier - fourier_hi.astype(jnp.float32)).astype(jnp.bfloat16)
    portion = lax.all_to_all(fields, "lon", split_axis=3, concat_axis=2, tiled=True)
    spectrum = jnp.einsum("bjkc,kf->jfbc", portion, fourier_hi, preferred_element_type=jnp.float32)
    spectrum = spectrum + jnp.einsum(
        "bjkc,kf->jfbc", portion, fourier_lo, preferred_element_type=jnp.float32
    )
    owned = lax.all_to_all(spectrum, "lon", split_axis=1, concat_axis=3, tiled=True)
    spectral = owned.reshape(owned.shape[0], column_rows, channels)
    wave_global = lax.axis_index("lon") * wave_dev + jnp.arange(wave_dev, dtype=jnp.int32)
    degree_ids = jnp.arange(degrees, dtype=jnp.int32)
    keep = degree_ids[None, None, :] >= wave_global[None, :, None]
    basis = jnp.where(keep, legendre, jnp.float32(0.0))
    spectral_waves = spectral.reshape(lat_rows, wave_dev, column_width)
    summed = lax.psum_scatter(
        jnp.einsum("jml,jmq->lmq", basis, spectral_waves, precision=lax.Precision.HIGHEST),
        "lat",
        scatter_dimension=0,
        tiled=True,
    )
    coef = summed.reshape(degree_dev, column_rows, channels)
    coef_bf = coef.astype(jnp.bfloat16)
    mixed = jnp.einsum("lrc,lcd->lrd", coef_bf, mixing, preferred_element_type=jnp.float32)
    mixed = mixed.astype(jnp.bfloat16).reshape(degree_dev, wave_dev, 2, samples, channels)
    cot_rows = cotangent.reshape(degree_dev, column_rows, channels)
    weight_grad = lax.psum_scatter(
        jnp.einsum("lrc,lrd->cld", coef_bf, cot_rows, preferred_element_type=jnp.float32),
        "lon",
        scatter_dimension=0,
        tiled=True,
    )
    return (mixed, weight_grad)


def tile_slots(degrees):
    slots = []
    for group in range(degrees // 2 + 1):
        for place in range(degrees):
            if place >= group:
                slots.append((group, place))
            elif group < degrees - group:
                slots.append((degrees - group, place + degrees - group))
            else:
                slots.append(None)
    return slots


def packed_tiles(wave_dev, index, cots, legendre_ref, table_ref):
    degrees, rows = legendre_ref.shape[1:]
    slots = tile_slots(degrees)
    row = lax.broadcasted_iota(jnp.int32, (TILE, LANES), 0)
    zeros = jnp.zeros((TILE, LANES), F32)
    owned = [index == owner for owner in range((degrees - 1) // wave_dev + 1)]

    def cotangent(slot):
        if slot is None:
            return zeros
        wave, degree = slot
        at = (degree * wave_dev + wave % wave_dev) * TILE
        return jnp.where(owned[wave // wave_dev], cots[at : at + TILE], 0.0)

    upper = row < TILE // 2
    parts = ([], [])
    for pair in range(len(slots) // 2):
        one, two = cotangent(slots[2 * pair]), cotangent(slots[2 * pair + 1])
        parts[0].append(jnp.where(upper, one, pltpu.roll(two, TILE // 2, 0)))
        parts[1].append(jnp.where(upper, pltpu.roll(one, TILE // 2, 0), two))

    table_ref[...] = jnp.zeros(table_ref.shape, F32)
    table_ref[:, :, pl.ds(0, rows)] = legendre_ref[...]

    def basis(wave):
        block = jnp.where(owned[wave // wave_dev], table_ref[wave % wave_dev], 0.0)
        return jnp.where(row >= wave, block, 0.0)

    table = jnp.zeros((degrees, 2 * LANES), F32)
    for group in range(degrees // 2 + 1):
        block = basis(group)
        if 0 < group < degrees - group:
            rest = pltpu.roll(basis(degrees - group), group, 0)
            block = block + pltpu.roll(rest, rows, 1)
        block = jnp.concatenate([block, zeros], axis=1)
        table = table + (pltpu.roll(block, 2 * rows * group, 1) if group else block)
    high = table.astype(BF16).astype(F32)

    half = len(slots) // 4
    whole = []
    for tiles in parts:
        lanes = [tiles[lane * half : (lane + 1) * half] for lane in range(2)]
        cots = jnp.concatenate([jnp.concatenate(lane, axis=0) for lane in lanes], axis=1)
        whole.append(jnp.concatenate([cots, high, table - high], axis=0))
    return whole


def side_of(index, lon_count):
    side = index
    for bit in range(1, lon_count.bit_length() - 2):
        side = side ^ (index >> bit)
    return side & 1


def fourier_kernel(
    lon_count,
    where_ref,
    fields_ref,
    legendre_ref,
    cot_ref,
    *refs,
):
    keep_refs, send_refs = refs[:CHAINS], refs[CHAINS : 2 * CHAINS]
    grid_ref, values_ref, cots_ref, total_ref, table_ref, sems = refs[2 * CHAINS :]
    channels = fields_ref.shape[2]
    wave_dev, degrees, rows = legendre_ref.shape
    cells = fields_ref.shape[1] // rows
    parts = 2 * degrees
    spec_rows = parts * rows
    nlon_total = cells * lon_count
    index = where_ref[0]
    side = side_of(index, lon_count)
    copies = [
        pltpu.make_async_copy(fields_ref.at[sample], grid_ref.at[k], sems.at[k])
        for k, sample in enumerate((1 - side, side))
    ]
    for copy in copies:
        copy.start()
    owns = index < (degrees - 1) // wave_dev + 1
    others = [
        pltpu.make_async_copy(legendre_ref, values_ref, sems.at[2]),
        pltpu.make_async_copy(cot_ref, cots_ref, sems.at[3]),
    ]

    @pl.when(owns)
    def _():
        for copy in others:
            copy.start()

    width = TILE * cells
    column = lax.broadcasted_iota(jnp.int32, (parts, width), 1)
    part = lax.broadcasted_iota(jnp.int32, (parts, width), 0)
    cell = index * cells + lax.rem(column, cells)
    turn = lax.rem(cell * (part // 2) + lax.rem(part, 2) * (nlon_total // 4), nlon_total)
    wave = jnp.cos(turn.astype(F32) * (2.0 * math.pi / nlon_total)) * (1.0 / nlon_total**0.5)
    spread = (parts, TILE, width)
    own_row = (
        lax.broadcasted_iota(jnp.int32, spread, 2) // cells
        == lax.broadcasted_iota(jnp.int32, spread, 1)
    )
    wave = jnp.where(own_row, jnp.broadcast_to(wave[:, None, :], spread), 0.0)
    wave = wave.reshape(parts * TILE, width)
    wave_hi = wave.astype(BF16)
    wave_lo = (wave - wave_hi.astype(F32)).astype(BF16)
    size = total_ref.shape[0] // CHAINS
    packed = total_ref.shape[0] - spec_rows
    rest = pl.ds(size - packed, packed)

    @pl.when(owns)
    def _():
        for copy in others:
            copy.wait()
        cots = cots_ref[...].astype(F32)
        real, imag = packed_tiles(wave_dev, index, cots, values_ref, table_ref)
        keep_refs[-1][rest, :] = jnp.where(side == 0, real, imag)
        total_ref[pl.ds(spec_rows, packed), :] = jnp.where(side == 0, imag, real)

    @pl.when(jnp.logical_not(owns))
    def _():
        keep_refs[-1][rest, :] = jnp.zeros((packed, channels), F32)
        total_ref[pl.ds(spec_rows, packed), :] = jnp.zeros((packed, channels), F32)

    for copy in copies:
        copy.wait()
    for k, first in [(k, first) for k in range(2) for first in range(0, rows, TILE)]:
        grid = grid_ref[k, pl.ds(first * cells, width), :]
        sums = jnp.dot(wave_hi, grid, preferred_element_type=F32)
        sums = sums + jnp.dot(wave_lo, grid, preferred_element_type=F32)
        for part in range(parts):
            tile = sums[part * TILE : (part + 1) * TILE]
            at = part * rows + first
            if k == 0:
                total_ref[pl.ds(at, TILE), :] = tile
            else:
                keep_refs[at // size][pl.ds(at % size, TILE), :] = tile
        if k == 0 and first + TILE == rows:
            for chain, send_ref in enumerate(send_refs):
                send_ref[...] = total_ref[pl.ds(chain * size, size), :].astype(BF16)


def legendre_kernel(rows, *refs):
    degrees = TILE
    groups = degrees // 2 + 1
    out_ref = refs[-1]
    sums = [
        refs[2 * chain][...] + refs[2 * chain + 1][...].astype(F32) for chain in range(CHAINS)
    ]
    spec_rows = 2 * degrees * rows
    spec = jnp.concatenate(sums, axis=0)
    packed = groups * 2 * degrees
    table = spec[spec_rows + packed :]
    spec_hi = spec[:spec_rows].astype(BF16).astype(F32)
    spec_lo = spec[:spec_rows] - spec_hi
    coefs = []
    for part in range(2):
        for group in range(groups):
            basis = table[:, 2 * rows * group : 2 * rows * (group + 1)].astype(BF16)
            partner = degrees - group if 0 < group < degrees - group else group
            low = (2 * group + part) * rows
            high = (2 * partner + part) * rows
            block, rest = (
                jnp.concatenate([half[low : low + rows], half[high : high + rows]], axis=0)
                for half in (spec_hi, spec_lo)
            )
            sums = jnp.dot(basis, block.astype(BF16), preferred_element_type=F32)
            more = jnp.dot(basis[:degrees], rest.astype(BF16), preferred_element_type=F32)
            coefs.append(sums[:degrees] + sums[degrees:] + more)
    coefs.append(spec[spec_rows : spec_rows + packed])
    out_ref[...] = jnp.concatenate(coefs, axis=0).astype(BF16)


def mixing_kernel(
    lon_count, wave_dev, samples, where_ref, mine_ref, other_ref, mixing_ref, mixed_ref, grad_ref, cot_ref, out_ref
):
    degrees, channels = mixing_ref.shape[:2]
    groups = degrees // 2 + 1
    slots = groups * degrees
    terms = 2 * samples * slots
    index = where_ref[0]
    side = side_of(index, lon_count)
    mine, other = mine_ref[...].astype(F32), other_ref[...].astype(F32)
    held = [jnp.where(side == k, mine, other) for k in range(2)]
    coef = [held[sample][part * slots : (part + 1) * slots] for part in range(2) for sample in range(2)]
    coef = jnp.concatenate(coef, axis=0).astype(BF16)
    cots = []
    for part in range(2):
        packed = held[part][2 * slots :]
        for lane in range(2):
            half = packed[:, lane * LANES : (lane + 1) * LANES]
            cot_ref[part, pl.ds(lane * packed.shape[0], packed.shape[0]), :] = half
        for sample in range(samples):
            halves = [
                cot_ref[part, pl.ds(2 * lane + sample, slots, stride=2 * samples), :]
                for lane in range(2)
            ]
            cots.append(jnp.concatenate(halves, axis=1))
    cot = jnp.concatenate(cots, axis=0).astype(BF16)

    block = 2 * TILE
    shape = (block, terms)
    row = lax.broadcasted_iota(jnp.int32, shape, 0)
    term = lax.broadcasted_iota(jnp.int32, shape, 1)
    wave = index * wave_dev + row // 2
    tile = jnp.where(wave < groups, wave * degrees, (degrees - wave) * degrees - wave)
    base = row % 2 * (samples * slots) + tile
    chosen = []
    for degree in range(degrees):
        for sample in range(samples):
            hit = jnp.where(wave <= degree, base + (sample * slots + degree), -1)
            chosen.append(jnp.where(term == hit, 1.0, 0.0).astype(BF16))
    chosen = jnp.concatenate(chosen, axis=0)
    lhs = jnp.dot(chosen, coef, preferred_element_type=F32).astype(BF16)
    count = 2 * wave_dev
    for degree in range(degrees):
        at = degree * samples * block
        mixed = jnp.dot(
            lhs[at : at + samples * block], mixing_ref[degree], preferred_element_type=F32
        )
        for sample in range(samples):
            for lane in range(2):
                part = mixed[sample * block : sample * block + count, lane * LANES : (lane + 1) * LANES]
                at = degree * 2 * samples * count + 2 * lane + sample
                out_ref[pl.ds(at, count, stride=2 * samples), :] = part
    mixed_ref[...] = out_ref[...].astype(BF16)

    own = grad_ref.shape[0]
    channel = lax.broadcasted_iota(jnp.int32, (own, channels), 1)
    row = lax.broadcasted_iota(jnp.int32, (own, channels), 0)
    pick = jnp.where(channel == index * own + row, 1.0, 0.0).astype(BF16)
    turned = lax.dot_general(
        pick, coef, (((1,), (1,)), ((), ())), preferred_element_type=F32
    )
    shape = (degrees, terms)
    slot = lax.broadcasted_iota(jnp.int32, shape, 1) % slots
    place, group = slot % degrees, slot // degrees
    degree = jnp.where(place >= group, place, place + degrees - group)
    of_degree = degree == lax.broadcasted_iota(jnp.int32, shape, 0)
    turned = [jnp.where(of_degree, turned[k : k + 1], 0.0) for k in range(own)]
    turned = jnp.concatenate(turned, axis=0).astype(BF16)
    grad = jnp.dot(turned, cot, preferred_element_type=F32)
    grad_ref[...] = grad.reshape(own, degrees, channels)


def sparse_shards(fields, legendre, mixing, cotangent):
    samples, rows, cells, channels = fields.shape
    lon_count = lax.axis_size("lon")
    wave_dev, degrees = legendre.shape[1:]
    parts = 2 * degrees
    spec_rows = parts * rows
    packed_rows = (degrees // 2 + 1) * parts
    index = lax.axis_index("lon")
    where = index.reshape(1).astype(jnp.int32)
    whole = pl.BlockSpec(memory_space=pltpu.VMEM)
    scalar = pl.BlockSpec(memory_space=pltpu.SMEM)
    params = pltpu.CompilerParams(vmem_limit_bytes=VMEM_BYTES)

    def in_hbm(array):
        return pltpu.with_memory_space_constraint(array, pltpu.HBM)

    def exchange(array, *hops):
        pairs = [(i, i ^ hops[side_of(i, lon_count)]) for i in range(lon_count)]
        return lax.ppermute(array, "lon", pairs)

    size = (spec_rows + packed_rows + 2 * TILE) // CHAINS
    halves = cotangent.reshape(degrees, wave_dev, 2, samples, 2, LANES)
    halves = halves.transpose(0, 1, 2, 4, 3, 5).reshape(-1, LANES)
    grid = fields.reshape(samples, rows * cells, channels)
    far = pl.BlockSpec(memory_space=pltpu.HBM)
    outs = pl.pallas_call(
        functools.partial(fourier_kernel, lon_count),
        out_shape=(jax.ShapeDtypeStruct((size, channels), F32),) * CHAINS
        + (jax.ShapeDtypeStruct((size, channels), BF16),) * CHAINS,
        in_specs=[scalar, far, far, far],
        out_specs=(whole,) * (2 * CHAINS),
        scratch_shapes=[
            pltpu.VMEM((samples, rows * cells, channels), BF16),
            pltpu.VMEM((wave_dev, degrees, rows), F32),
            pltpu.VMEM(halves.shape, BF16),
            pltpu.VMEM((CHAINS * size, channels), F32),
            pltpu.VMEM((wave_dev, degrees, LANES), F32),
            pltpu.SemaphoreType.DMA((4,)),
        ],
        compiler_params=params,
    )(where, in_hbm(grid), in_hbm(legendre.transpose(1, 2, 0)), in_hbm(halves))

    accs = [
        keep + exchange(send, 1, 1).astype(F32)
        for keep, send in zip(outs[:CHAINS], outs[CHAINS:])
    ]
    for step, hops in enumerate(zip(*hop_orders(lon_count))):
        gots = [exchange(acc.astype(BF16), *hop) for acc, hop in zip(accs, hops)]
        if step < len(hop_orders(lon_count)[0]) - 1:
            accs = [acc + got.astype(F32) for acc, got in zip(accs, gots)]
    pairs = [array for pair in zip(accs, gots) for array in pair]

    mine = pl.pallas_call(
        functools.partial(legendre_kernel, rows),
        out_shape=jax.ShapeDtypeStruct((2 * packed_rows, channels), BF16),
        in_specs=[whole] * (2 * CHAINS),
        out_specs=whole,
        compiler_params=params,
    )(*pairs)
    other = exchange(mine, 1, 1)

    block_rows = 2 * wave_dev * samples
    mixed, grad = pl.pallas_call(
        functools.partial(mixing_kernel, lon_count, wave_dev, samples),
        out_shape=(
            jax.ShapeDtypeStruct((degrees * block_rows * 2, LANES), BF16),
            jax.ShapeDtypeStruct((channels // lon_count, degrees, channels), F32),
        ),
        in_specs=[scalar] + [whole] * 3,
        out_specs=(whole, whole),
        scratch_shapes=[
            pltpu.VMEM((2, packed_rows * 2, LANES), F32),
            pltpu.VMEM((degrees * block_rows * 2, LANES), F32),
        ],
        compiler_params=params,
    )(where, mine, other, mixing)
    mixed = mixed.reshape(degrees, wave_dev, 2, 2, samples, LANES).transpose(0, 1, 2, 4, 3, 5)
    return mixed.reshape(degrees, wave_dev, 2, samples, channels), grad


def hop_orders(lon_count):
    bits = [1 << k for k in range(1, lon_count.bit_length() - 1)]
    bits[-1] += bits[-2]
    bits = [bit + 1 for bit in bits]
    half = len(bits) // 2
    near, far = bits[:half], bits[half:]
    one = [hop for pair in zip(near, far) for hop in pair]
    two = [hop for pair in zip(far, near) for hop in pair]
    chain_a = list(zip(one, two))
    chain_b = list(zip(one[half:] + one[:half][::-1], two[half:] + two[:half][::-1]))
    return chain_a, chain_b, list(zip(two, one))


def few_waves(mesh, fields, legendre):
    samples, rows, longitudes, channels = fields.shape
    waves, degrees = legendre.shape[1:]
    count = mesh.shape["lon"]
    return (
        mesh.shape["lat"] == 1
        and samples == 2
        and count >= 8
        and count & (count - 1) == 0
        and count.bit_length() % 2 == 0
        and degrees == TILE
        and degrees <= waves
        and rows % TILE == 0
        and (2 * degrees * (rows + degrees // 2 + 1) + 2 * TILE) % (2 * TILE * CHAINS) == 0
        and longitudes // count % 2 == 0
        and 2 * rows * (degrees // 2 + 1) <= channels
        and channels == 2 * LANES
        and channels // count == TILE
        and longitudes % 4 == 0
        and (4 * waves // count) % TILE == 0
    )


def solution(mesh):
    placed = (
        P(None, "lat", "lon", None),
        P("lat", "lon", None),
        P("lat", None, None),
        P("lat", "lon", None, None, None),
    )

    def program(fields, legendre, mixing, cotangent):
        body = sparse_shards if few_waves(mesh, fields, legendre) else dense_shards
        return jax.shard_map(
            body,
            mesh=mesh,
            in_specs=placed,
            out_specs=(P("lat", "lon", None, None, None), P("lon", "lat", None)),
            check_vma=False,
        )(fields, legendre, mixing, cotangent)

    return program
```

```python
import functools
import math

import jax
import jax.numpy as jnp
from jax import lax
from jax.experimental import pallas as pl
from jax.experimental.pallas import tpu as pltpu
from jax.sharding import PartitionSpec as P

F32 = jnp.float32
BF16 = jnp.bfloat16
TILE = 8
LANES = 128
VMEM_BYTES = 32 * 1024 * 1024


def dense_shards(fields, legendre, mixing, cotangent):
    samples = fields.shape[0]
    lat_rows = fields.shape[1]
    lon_cells = fields.shape[2]
    channels = fields.shape[3]
    lon_count = lax.axis_size("lon")
    lat_count = lax.axis_size("lat")
    nlon_total = lon_cells * lon_count
    wave_dev = legendre.shape[1]
    wave_total = wave_dev * lon_count
    degrees = legendre.shape[2]
    degree_dev = degrees // lat_count
    column_rows = 2 * wave_dev * samples
    column_width = 2 * samples * channels
    positions = jnp.arange(nlon_total, dtype=jnp.int32)
    wavenums = jnp.arange(wave_total, dtype=jnp.int32)
    phase = (positions[:, None] * wavenums[None, :] % nlon_total).astype(jnp.float32) * (
        2.0 * math.pi / nlon_total
    )
    fourier = jnp.stack([jnp.cos(phase), -jnp.sin(phase)], axis=2).reshape(
        nlon_total, 2 * wave_total
    )
    fourier = fourier * (1.0 / nlon_total**0.5)
    fourier_hi = fourier.astype(jnp.bfloat16)
    fourier_lo = (fourier - fourier_hi.astype(jnp.float32)).astype(jnp.bfloat16)
    portion = lax.all_to_all(fields, "lon", split_axis=3, concat_axis=2, tiled=True)
    spectrum = jnp.einsum("bjkc,kf->jfbc", portion, fourier_hi, preferred_element_type=jnp.float32)
    spectrum = spectrum + jnp.einsum(
        "bjkc,kf->jfbc", portion, fourier_lo, preferred_element_type=jnp.float32
    )
    owned = lax.all_to_all(spectrum, "lon", split_axis=1, concat_axis=3, tiled=True)
    spectral = owned.reshape(owned.shape[0], column_rows, channels)
    wave_global = lax.axis_index("lon") * wave_dev + jnp.arange(wave_dev, dtype=jnp.int32)
    degree_ids = jnp.arange(degrees, dtype=jnp.int32)
    keep = degree_ids[None, None, :] >= wave_global[None, :, None]
    basis = jnp.where(keep, legendre, jnp.float32(0.0))
    spectral_waves = spectral.reshape(lat_rows, wave_dev, column_width)
    summed = lax.psum_scatter(
        jnp.einsum("jml,jmq->lmq", basis, spectral_waves, precision=lax.Precision.HIGHEST),
        "lat",
        scatter_dimension=0,
        tiled=True,
    )
    coef = summed.reshape(degree_dev, column_rows, channels)
    coef_bf = coef.astype(jnp.bfloat16)
    mixed = jnp.einsum("lrc,lcd->lrd", coef_bf, mixing, preferred_element_type=jnp.float32)
    mixed = mixed.astype(jnp.bfloat16).reshape(degree_dev, wave_dev, 2, samples, channels)
    cot_rows = cotangent.reshape(degree_dev, column_rows, channels)
    weight_grad = lax.psum_scatter(
        jnp.einsum("lrc,lrd->cld", coef_bf, cot_rows, preferred_element_type=jnp.float32),
        "lon",
        scatter_dimension=0,
        tiled=True,
    )
    return (mixed, weight_grad)


def tile_slots(degrees):
    slots = []
    for group in range(degrees // 2 + 1):
        for place in range(degrees):
            if place >= group:
                slots.append((group, place))
            elif group < degrees - group:
                slots.append((degrees - group, place + degrees - group))
            else:
                slots.append(None)
    return slots


def packed_tiles(wave_dev, index, cots, legendre_ref, table_ref):
    degrees, rows = legendre_ref.shape[1:]
    slots = tile_slots(degrees)
    row = lax.broadcasted_iota(jnp.int32, (TILE, LANES), 0)
    zeros = jnp.zeros((TILE, LANES), F32)
    owned = [index == owner for owner in range((degrees - 1) // wave_dev + 1)]

    def cotangent(slot):
        if slot is None:
            return zeros
        wave, degree = slot
        at = (degree * wave_dev + wave % wave_dev) * TILE
        return jnp.where(owned[wave // wave_dev], cots[at : at + TILE], 0.0)

    upper = row < TILE // 2
    parts = ([], [])
    for pair in range(len(slots) // 2):
        one, two = cotangent(slots[2 * pair]), cotangent(slots[2 * pair + 1])
        parts[0].append(jnp.where(upper, one, pltpu.roll(two, TILE // 2, 0)))
        parts[1].append(jnp.where(upper, pltpu.roll(one, TILE // 2, 0), two))

    table_ref[...] = jnp.zeros(table_ref.shape, F32)
    table_ref[:, :, pl.ds(0, rows)] = legendre_ref[...]

    def basis(wave):
        block = jnp.where(owned[wave // wave_dev], table_ref[wave % wave_dev], 0.0)
        return jnp.where(row >= wave, block, 0.0)

    table = jnp.zeros((degrees, 2 * LANES), F32)
    for group in range(degrees // 2 + 1):
        block = basis(group)
        if 0 < group < degrees - group:
            rest = pltpu.roll(basis(degrees - group), group, 0)
            block = block + pltpu.roll(rest, rows, 1)
        block = jnp.concatenate([block, zeros], axis=1)
        table = table + (pltpu.roll(block, 2 * rows * group, 1) if group else block)
    high = table.astype(BF16).astype(F32)

    half = len(slots) // 4
    whole = []
    for tiles in parts:
        lanes = [tiles[lane * half : (lane + 1) * half] for lane in range(2)]
        cots = jnp.concatenate([jnp.concatenate(lane, axis=0) for lane in lanes], axis=1)
        whole.append(jnp.concatenate([cots, high, table - high], axis=0))
    return whole


def side_of(index, lon_count):
    side = index
    for bit in range(1, lon_count.bit_length() - 2):
        side = side ^ (index >> bit)
    return side & 1


def fourier_kernel(
    lon_count,
    where_ref,
    fields_ref,
    legendre_ref,
    cot_ref,
    first_ref,
    second_ref,
    first_send_ref,
    second_send_ref,
    grid_ref,
    values_ref,
    cots_ref,
    total_ref,
    table_ref,
    sems,
):
    channels = fields_ref.shape[2]
    wave_dev, degrees, rows = legendre_ref.shape
    cells = fields_ref.shape[1] // rows
    parts = 2 * degrees
    spec_rows = parts * rows
    nlon_total = cells * lon_count
    index = where_ref[0]
    side = side_of(index, lon_count)
    copies = [
        pltpu.make_async_copy(fields_ref.at[sample], grid_ref.at[k], sems.at[k])
        for k, sample in enumerate((1 - side, side))
    ]
    for copy in copies:
        copy.start()
    owns = index < (degrees - 1) // wave_dev + 1
    others = [
        pltpu.make_async_copy(legendre_ref, values_ref, sems.at[2]),
        pltpu.make_async_copy(cot_ref, cots_ref, sems.at[3]),
    ]

    @pl.when(owns)
    def _():
        for copy in others:
            copy.start()

    width = TILE * cells
    column = lax.broadcasted_iota(jnp.int32, (parts, width), 1)
    part = lax.broadcasted_iota(jnp.int32, (parts, width), 0)
    cell = index * cells + lax.rem(column, cells)
    turn = lax.rem(cell * (part // 2) + lax.rem(part, 2) * (nlon_total // 4), nlon_total)
    wave = jnp.cos(turn.astype(F32) * (2.0 * math.pi / nlon_total)) * (1.0 / nlon_total**0.5)
    spread = (parts, TILE, width)
    own_row = (
        lax.broadcasted_iota(jnp.int32, spread, 2) // cells
        == lax.broadcasted_iota(jnp.int32, spread, 1)
    )
    wave = jnp.where(own_row, jnp.broadcast_to(wave[:, None, :], spread), 0.0)
    wave = wave.reshape(parts * TILE, width)
    wave_hi = wave.astype(BF16)
    wave_lo = (wave - wave_hi.astype(F32)).astype(BF16)
    cut = first_ref.shape[0] // rows
    kept = (parts - cut) * rows
    rest = pl.ds(kept, second_ref.shape[0] - kept)

    @pl.when(owns)
    def _():
        for copy in others:
            copy.wait()
        cots = cots_ref[...].astype(F32)
        real, imag = packed_tiles(wave_dev, index, cots, values_ref, table_ref)
        second_ref[rest, :] = jnp.where(side == 0, real, imag)
        total_ref[pl.ds(spec_rows, rest.size), :] = jnp.where(side == 0, imag, real)

    @pl.when(jnp.logical_not(owns))
    def _():
        second_ref[rest, :] = jnp.zeros((rest.size, channels), F32)
        total_ref[pl.ds(spec_rows, rest.size), :] = jnp.zeros((rest.size, channels), F32)

    for copy in copies:
        copy.wait()
    for k, first in [(k, first) for k in range(2) for first in range(0, rows, TILE)]:
        grid = grid_ref[k, pl.ds(first * cells, width), :]
        sums = jnp.dot(wave_hi, grid, preferred_element_type=F32)
        sums = sums + jnp.dot(wave_lo, grid, preferred_element_type=F32)
        for part in range(parts):
            tile = sums[part * TILE : (part + 1) * TILE]
            if k == 0:
                total_ref[pl.ds(part * rows + first, TILE), :] = tile
            elif part < cut:
                first_ref[pl.ds(part * rows + first, TILE), :] = tile
            else:
                second_ref[pl.ds((part - cut) * rows + first, TILE), :] = tile
        if k == 0 and first + TILE == rows:
            first_send_ref[...] = total_ref[pl.ds(0, cut * rows), :].astype(BF16)
            after = pl.ds(cut * rows, second_send_ref.shape[0])
            second_send_ref[...] = total_ref[after, :].astype(BF16)


def legendre_kernel(
    rows, first_ref, first_got_ref, second_ref, second_got_ref, out_ref
):
    degrees = TILE
    groups = degrees // 2 + 1
    first = first_ref[...] + first_got_ref[...].astype(F32)
    second = second_ref[...] + second_got_ref[...].astype(F32)
    spec_rows = 2 * degrees * rows
    spec = jnp.concatenate([first, second], axis=0)
    packed = groups * 2 * degrees
    table = spec[spec_rows + packed :]
    spec_hi = spec[:spec_rows].astype(BF16).astype(F32)
    spec_lo = spec[:spec_rows] - spec_hi
    coefs = []
    for part in range(2):
        for group in range(groups):
            basis = table[:, 2 * rows * group : 2 * rows * (group + 1)]
            partner = degrees - group if 0 < group < degrees - group else group
            low = (2 * group + part) * rows
            high = (2 * partner + part) * rows
            block, rest = (
                jnp.concatenate([half[low : low + rows], half[high : high + rows]], axis=0)
                for half in (spec_hi, spec_lo)
            )
            last = jnp.concatenate([basis[:degrees], jnp.zeros_like(basis[:degrees])], axis=0)
            both = jnp.concatenate([basis, last], axis=1).astype(BF16)
            block = jnp.concatenate([block, rest], axis=0).astype(BF16)
            sums = jnp.dot(both, block, preferred_element_type=F32)
            coefs.append(sums[:degrees] + sums[degrees:])
    coefs.append(spec[spec_rows : spec_rows + packed])
    out_ref[...] = jnp.concatenate(coefs, axis=0).astype(BF16)


def mixing_kernel(
    lon_count, wave_dev, samples, where_ref, mine_ref, other_ref, mixing_ref, mixed_ref, grad_ref, cot_ref, out_ref
):
    degrees, channels = mixing_ref.shape[:2]
    groups = degrees // 2 + 1
    slots = groups * degrees
    terms = 2 * samples * slots
    index = where_ref[0]
    side = side_of(index, lon_count)
    mine, other = mine_ref[...].astype(F32), other_ref[...].astype(F32)
    held = [jnp.where(side == k, mine, other) for k in range(2)]
    coef = [held[sample][part * slots : (part + 1) * slots] for part in range(2) for sample in range(2)]
    coef = jnp.concatenate(coef, axis=0).astype(BF16)
    cots = []
    for part in range(2):
        packed = held[part][2 * slots :]
        for lane in range(2):
            half = packed[:, lane * LANES : (lane + 1) * LANES]
            cot_ref[part, pl.ds(lane * packed.shape[0], packed.shape[0]), :] = half
        for sample in range(samples):
            halves = [
                cot_ref[part, pl.ds(2 * lane + sample, slots, stride=2 * samples), :]
                for lane in range(2)
            ]
            cots.append(jnp.concatenate(halves, axis=1))
    cot = jnp.concatenate(cots, axis=0).astype(BF16)

    block = 2 * TILE
    shape = (block, terms)
    row = lax.broadcasted_iota(jnp.int32, shape, 0)
    term = lax.broadcasted_iota(jnp.int32, shape, 1)
    wave = index * wave_dev + row // 2
    tile = jnp.where(wave < groups, wave * degrees, (degrees - wave) * degrees - wave)
    base = row % 2 * (samples * slots) + tile
    chosen = []
    for degree in range(degrees):
        for sample in range(samples):
            hit = jnp.where(wave <= degree, base + (sample * slots + degree), -1)
            chosen.append(jnp.where(term == hit, 1.0, 0.0).astype(BF16))
    chosen = jnp.concatenate(chosen, axis=0)
    lhs = jnp.dot(chosen, coef, preferred_element_type=F32).astype(BF16)
    count = 2 * wave_dev
    for degree in range(degrees):
        at = degree * samples * block
        mixed = jnp.dot(
            lhs[at : at + samples * block], mixing_ref[degree], preferred_element_type=F32
        )
        for sample in range(samples):
            for lane in range(2):
                part = mixed[sample * block : sample * block + count, lane * LANES : (lane + 1) * LANES]
                at = degree * 2 * samples * count + 2 * lane + sample
                out_ref[pl.ds(at, count, stride=2 * samples), :] = part
    mixed_ref[...] = out_ref[...].astype(BF16)

    own = grad_ref.shape[0]
    channel = lax.broadcasted_iota(jnp.int32, (own, channels), 1)
    row = lax.broadcasted_iota(jnp.int32, (own, channels), 0)
    pick = jnp.where(channel == index * own + row, 1.0, 0.0).astype(BF16)
    turned = lax.dot_general(
        pick, coef, (((1,), (1,)), ((), ())), preferred_element_type=F32
    )
    shape = (degrees, terms)
    slot = lax.broadcasted_iota(jnp.int32, shape, 1) % slots
    place, group = slot % degrees, slot // degrees
    degree = jnp.where(place >= group, place, place + degrees - group)
    of_degree = degree == lax.broadcasted_iota(jnp.int32, shape, 0)
    turned = [jnp.where(of_degree, turned[k : k + 1], 0.0) for k in range(own)]
    turned = jnp.concatenate(turned, axis=0).astype(BF16)
    grad = jnp.dot(turned, cot, preferred_element_type=F32)
    grad_ref[...] = grad.reshape(own, degrees, channels)


def sparse_shards(fields, legendre, mixing, cotangent):
    samples, rows, cells, channels = fields.shape
    lon_count = lax.axis_size("lon")
    wave_dev, degrees = legendre.shape[1:]
    parts = 2 * degrees
    spec_rows = parts * rows
    packed_rows = (degrees // 2 + 1) * parts
    index = lax.axis_index("lon")
    where = index.reshape(1).astype(jnp.int32)
    whole = pl.BlockSpec(memory_space=pltpu.VMEM)
    scalar = pl.BlockSpec(memory_space=pltpu.SMEM)
    params = pltpu.CompilerParams(vmem_limit_bytes=VMEM_BYTES)

    def in_hbm(array):
        return pltpu.with_memory_space_constraint(array, pltpu.HBM)

    def exchange(array, *hops):
        pairs = [(i, i ^ hops[side_of(i, lon_count)]) for i in range(lon_count)]
        return lax.ppermute(array, "lon", pairs)

    cut = (parts // 2 + 3) * rows
    rest = spec_rows - cut + packed_rows + 2 * TILE
    halves = cotangent.reshape(degrees, wave_dev, 2, samples, 2, LANES)
    halves = halves.transpose(0, 1, 2, 4, 3, 5).reshape(-1, LANES)
    grid = fields.reshape(samples, rows * cells, channels)
    far = pl.BlockSpec(memory_space=pltpu.HBM)
    acc_a, acc_b, send_a, send_b = pl.pallas_call(
        functools.partial(fourier_kernel, lon_count),
        out_shape=(
            jax.ShapeDtypeStruct((cut, channels), F32),
            jax.ShapeDtypeStruct((rest, channels), F32),
            jax.ShapeDtypeStruct((cut, channels), BF16),
            jax.ShapeDtypeStruct((rest, channels), BF16),
        ),
        in_specs=[scalar, far, far, far],
        out_specs=(whole, whole, whole, whole),
        scratch_shapes=[
            pltpu.VMEM((samples, rows * cells, channels), BF16),
            pltpu.VMEM((wave_dev, degrees, rows), F32),
            pltpu.VMEM(halves.shape, BF16),
            pltpu.VMEM((cut + rest, channels), F32),
            pltpu.VMEM((wave_dev, degrees, LANES), F32),
            pltpu.SemaphoreType.DMA((4,)),
        ],
        compiler_params=params,
    )(where, in_hbm(grid), in_hbm(legendre.transpose(1, 2, 0)), in_hbm(halves))

    acc_a = acc_a + exchange(send_a, 1, 1).astype(F32)
    acc_b = acc_b + exchange(send_b, 1, 1).astype(F32)
    orders_a, orders_b = hop_orders(lon_count)
    for step, (hops_a, hops_b) in enumerate(zip(orders_a, orders_b)):
        got_a = exchange(acc_a.astype(BF16), *hops_a)
        got_b = exchange(acc_b.astype(BF16), *hops_b)
        if step < len(orders_a) - 1:
            acc_a = acc_a + got_a.astype(F32)
            acc_b = acc_b + got_b.astype(F32)

    mine = pl.pallas_call(
        functools.partial(legendre_kernel, rows),
        out_shape=jax.ShapeDtypeStruct((2 * packed_rows, channels), BF16),
        in_specs=[whole] * 4,
        out_specs=whole,
        compiler_params=params,
    )(acc_a, got_a, acc_b, got_b)
    other = exchange(mine, 1, 1)

    block_rows = 2 * wave_dev * samples
    mixed, grad = pl.pallas_call(
        functools.partial(mixing_kernel, lon_count, wave_dev, samples),
        out_shape=(
            jax.ShapeDtypeStruct((degrees * block_rows * 2, LANES), BF16),
            jax.ShapeDtypeStruct((channels // lon_count, degrees, channels), F32),
        ),
        in_specs=[scalar] + [whole] * 3,
        out_specs=(whole, whole),
        scratch_shapes=[
            pltpu.VMEM((2, packed_rows * 2, LANES), F32),
            pltpu.VMEM((degrees * block_rows * 2, LANES), F32),
        ],
        compiler_params=params,
    )(where, mine, other, mixing)
    mixed = mixed.reshape(degrees, wave_dev, 2, 2, samples, LANES).transpose(0, 1, 2, 4, 3, 5)
    return mixed.reshape(degrees, wave_dev, 2, samples, channels), grad


def hop_orders(lon_count):
    bits = [1 << k for k in range(1, lon_count.bit_length() - 1)]
    bits[-1] += bits[-2]
    bits = [bit + 1 for bit in bits]
    half = len(bits) // 2
    near, far = bits[:half], bits[half:]
    one = [hop for pair in zip(near, far) for hop in pair]
    two = [hop for pair in zip(far, near) for hop in pair]
    chain_a = list(zip(one, two))
    chain_b = list(zip(one[half:] + one[:half][::-1], two[half:] + two[:half][::-1]))
    return chain_a, chain_b


def few_waves(mesh, fields, legendre):
    samples, rows, longitudes, channels = fields.shape
    waves, degrees = legendre.shape[1:]
    count = mesh.shape["lon"]
    return (
        mesh.shape["lat"] == 1
        and samples == 2
        and count >= 8
        and count & (count - 1) == 0
        and count.bit_length() % 2 == 0
        and degrees == TILE
        and degrees <= waves
        and rows % TILE == 0
        and longitudes // count % 2 == 0
        and 2 * rows * (degrees // 2 + 1) <= channels
        and channels == 2 * LANES
        and channels // count == TILE
        and longitudes % 4 == 0
        and (4 * waves // count) % TILE == 0
    )


def solution(mesh):
    placed = (
        P(None, "lat", "lon", None),
        P("lat", "lon", None),
        P("lat", None, None),
        P("lat", "lon", None, None, None),
    )

    def program(fields, legendre, mixing, cotangent):
        body = sparse_shards if few_waves(mesh, fields, legendre) else dense_shards
        return jax.shard_map(
            body,
            mesh=mesh,
            in_specs=placed,
            out_specs=(P("lat", "lon", None, None, None), P("lon", "lat", None)),
            check_vma=False,
        )(fields, legendre, mixing, cotangent)

    return program
```
